1024 devices in a mesh: rep: 32 (over y, z_hi, x), exp: 32 (over z_lo, core).
Axes of the slice: x: 4, y: 4, z: 32 (z_hi: 2, z_lo: 16; z = z_hi * 16 + z_lo), core: 2. Of those that a mesh axis runs over, the one named last changes fastest.
Arguments:
- tokens: bfloat16 [64, 256, 1280], P('exp'), may hold values from -6 to 6
- slot_proj: bfloat16 [1280, 64], replicated
- in_weight: bfloat16 [64, 1280, 5120], P('exp', None, 'rep'), may hold values from -0.15625 to 0.15625
- out_weight: bfloat16 [64, 5120, 1280], P('exp', 'rep'), may hold values from -0.078125 to 0.078125
- out_grad: bfloat16 [64, 256, 1280], P('exp'), may hold values from -6 to 6
Outputs:
- mixed: bfloat16 [64, 256, 1280], P('exp')
- token_grad: bfloat16 [64, 256, 1280], P('exp')
- proj_grad: bfloat16 [1280, 64], replicated
- in_weight_grad: bfloat16 [64, 1280, 5120], P('exp', None, 'rep')
- out_weight_grad: bfloat16 [64, 5120, 1280], P('exp', 'rep')
The draws below stay inside these ranges and needn't reach their ends.
All inputs are finite; a program needn't handle non-finite values.
Results may differ from the reference program's by a relative error of at most 0.04.
Values may be sent and summed in bfloat16 or wider, within the bound.
No kernel may reach another device: no remote copies, remote signals or barrier semaphores. Data moves between devices by JAX's collectives and lax.ppermute only.
A program may use at most 32 MiB of HBM per device.

```python
import jax
import jax.numpy as jnp
from jax import lax

D = 1280
FF = 5120
M = 256
IMAGES = 64
EXPERTS = 64


def draw_tokens(key, part):
    key = jax.random.fold_in(key, 3)
    values = jax.random.truncated_normal(key, -4.0, 4.0, (IMAGES, M, D), jnp.float32)
    return values.astype(jnp.bfloat16)


def draw_slot_proj(key, part):
    key = jax.random.fold_in(key, 7)
    values = jax.random.truncated_normal(key, -4.0, 4.0, (D, EXPERTS), jnp.float32) * (3.0 * D ** (-0.5))
    return values.astype(jnp.bfloat16)


def levels(key, shape, cuts, smallest, top_value):
    gain = 1.0
    for position, blocks in cuts:
        heights = jax.random.uniform(jax.random.fold_in(jax.random.fold_in(key, 6), position), (blocks,), jnp.float32, smallest / len(cuts), top_value / len(cuts))
        gain = gain * jnp.repeat(jnp.exp(heights), shape[position] // blocks).reshape((-1,) + (1,) * (len(shape) - 1 - position))
    return gain


def scatter_about(key, dims, spread, bound, cuts=(), kind=jnp.bfloat16):
    factor_of = levels(key, dims, cuts, -0.22, 0.18) if cuts else 1.0
    values = jax.random.normal(key, dims, jnp.float32) * spread * factor_of
    return jnp.minimum(jnp.maximum(values, -bound), bound).astype(kind)


def setup_inputs(seed: int = 0) -> dict:
    streams_of = jax.random.split(jax.random.key(seed), 6)
    return {
        "tokens": draw_tokens(jax.random.fold_in(streams_of[5], 71), 0),
        "slot_proj": draw_slot_proj(jax.random.fold_in(streams_of[5], 71), 0),
        "in_weight": scatter_about(streams_of[2], (EXPERTS, D, FF), D ** -0.5, 0.15625, ((0, 32), (2, 32))),
        "out_weight": scatter_about(streams_of[3], (EXPERTS, FF, D), FF ** -0.5, 0.078125, ((0, 32), (1, 32))),
        "out_grad": scatter_about(streams_of[4], (IMAGES, M, D), 1.0, 6.0, ((0, 32),)),
    }


def smooth(values):
    return jax.nn.gelu(values, approximate=True)

def rounded(values):
    return lax.optimization_barrier(values.astype(jnp.bfloat16)).astype(jnp.float32)

def expert_step(packed):
    slot_e, in_e, out_e, grad_e = packed
    pre_act = jnp.dot(slot_e, in_e, preferred_element_type=jnp.float32)
    activated, pullback = jax.vjp(smooth, pre_act)
    hidden = activated.astype(jnp.bfloat16)
    result = jnp.dot(hidden, out_e, preferred_element_type=jnp.float32).astype(jnp.bfloat16)
    hidden_grad = jnp.dot(grad_e, out_e.T, preferred_element_type=jnp.float32)
    pre_grad = pullback(hidden_grad)[0].astype(jnp.bfloat16)
    out_wgrad = jnp.dot(hidden.T, grad_e, preferred_element_type=jnp.float32).astype(jnp.bfloat16)
    in_wgrad = jnp.dot(slot_e.T, pre_grad, preferred_element_type=jnp.float32).astype(jnp.bfloat16)
    slot_grad = jnp.dot(pre_grad, in_e.T, preferred_element_type=jnp.float32).astype(jnp.bfloat16)
    return (result, out_wgrad, in_wgrad, slot_grad)

def reference(tokens, slot_proj, in_weight, out_weight, out_grad):
    token_rows = tokens.astype(jnp.float32)
    proj_rows = slot_proj.astype(jnp.float32)
    cot_rows = out_grad.astype(jnp.float32)
    logits = jnp.einsum('itd,de->ite', token_rows, proj_rows)
    dispatch = jax.nn.softmax(logits, axis=1)
    combine = jax.nn.softmax(logits, axis=2)
    dispatch_b = rounded(dispatch)
    combine_b = rounded(combine)
    slot_rows = jnp.einsum('ite,itd->ied', dispatch_b, token_rows).astype(jnp.bfloat16)
    expert_grad = jnp.einsum('ite,itd->ied', combine_b, cot_rows).astype(jnp.bfloat16)
    packed = (jnp.transpose(slot_rows, (1, 0, 2)), in_weight, out_weight, jnp.transpose(expert_grad, (1, 0, 2)))
    result, out_wgrad, in_wgrad, slot_back = lax.map(expert_step, packed)
    expert_out = jnp.transpose(result, (1, 0, 2)).astype(jnp.float32)
    slot_grad = jnp.transpose(slot_back, (1, 0, 2)).astype(jnp.float32)
    mixed = jnp.einsum('ite,ied->itd', combine_b, expert_out).astype(jnp.bfloat16)
    combine_grad = jnp.einsum('itd,ied->ite', cot_rows, expert_out)
    dispatch_grad = jnp.einsum('itd,ied->ite', token_rows, slot_grad)
    from_dispatch = dispatch * (dispatch_grad - lax.optimization_barrier(jnp.sum(dispatch * dispatch_grad, axis=1, keepdims=True)))
    from_combine = combine * (combine_grad - lax.optimization_barrier(jnp.sum(combine * combine_grad, axis=2, keepdims=True)))
    logit_grad = rounded(from_dispatch + from_combine)
    token_grad = (jnp.einsum('ite,ied->itd', dispatch_b, slot_grad) + jnp.einsum('ite,de->itd', logit_grad, proj_rows)).astype(jnp.bfloat16)
    proj_grad = jnp.einsum('itd,ite->de', token_rows, logit_grad).astype(jnp.bfloat16)
    return (mixed, token_grad, proj_grad, in_wgrad, out_wgrad)
```

```python
import jax
import jax.numpy as jnp
from jax import lax
from jax.sharding import Mesh, PartitionSpec as P

ALL = ("y", "zh", "x", "zq", "zr", "c")
PLANE = ("y", "x")
PLANE_CORES = ("y", "x", "c")
EXP = ("zq", "zr", "c")
REP = ("y", "zh", "x")
BF = jnp.bfloat16
F32 = jnp.float32


def signed(r):
    return r if r <= 8 else r - 16


def shifted(value, sign, extra=0):
    pairs = []
    for y in range(4):
        for x in range(4):
            for z in range(32):
                for c in range(2):
                    to = (z + sign * signed(4 * y + x) * (1 - 2 * c) + extra) % 32
                    source = (((y * 2 + z // 16) * 4 + x) * 16 + z % 16) * 2 + c
                    target = (((y * 2 + to // 16) * 4 + x) * 16 + to % 16) * 2 + c
                    pairs.append((source, target))
    return lax.ppermute(value, ALL, pairs)


def smooth(values):
    return jax.nn.gelu(values, approximate=True)


def picked(index, rows):
    choose = (index[:, None] == jnp.arange(rows.shape[0])[None, :]).astype(BF)
    return jnp.dot(choose, rows, preferred_element_type=F32).astype(BF)


def spread(rows):
    out = jnp.broadcast_to(rows[None], (16,) + rows.shape).reshape((32,) + rows.shape[1:])
    return lax.all_to_all(out, PLANE_CORES, 0, 0, tiled=True)


def gathered(value, axes, size):
    out = jnp.broadcast_to(value[None], (size,) + value.shape)
    return lax.all_to_all(out, axes, 0, 0, tiled=True)


def on_device(tokens, slot_proj, in_weight, out_weight, out_grad):
    width = tokens.shape[2]
    column = lax.axis_index("y") * 4 + lax.axis_index("x")
    core = lax.axis_index("c")
    z_lo = lax.axis_index("zq") * 4 + lax.axis_index("zr")
    mirror = 1 - 2 * core
    logits = jnp.einsum("itd,de->ite", tokens, slot_proj, preferred_element_type=F32)
    dispatch = jax.nn.softmax(logits, axis=1)
    combine = jax.nn.softmax(logits, axis=2)
    dispatch_b = dispatch.astype(BF)
    combine_b = combine.astype(BF)
    slot_rows = jnp.einsum("ite,itd->ied", dispatch_b, tokens, preferred_element_type=F32).astype(BF)
    expert_grad = jnp.einsum("ite,itd->ied", combine_b, out_grad, preferred_element_type=F32).astype(BF)
    both = jnp.concatenate([slot_rows.reshape(128, width), expert_grad.reshape(128, width)])
    row = jnp.arange(16)
    target = (z_lo + mirror * column) % 16
    wanted = (row // 4) % 2 * 128 + row % 2 * 64 + 4 * target + row // 8 * 2 + (row // 2) % 2
    sent = shifted(picked(wanted, both), 1)
    got = spread(sent.reshape(2, 8, width)).reshape(256, width)
    row = jnp.arange(256)
    order = (row // 2) % 32 * 8 + row // 64 * 2 + row % 2
    kinds = picked(order, got).reshape(2, 2, 64, width)
    got_slots, got_grads = kinds[0], kinds[1]
    pre_act = jnp.einsum("erd,edf->erf", got_slots, in_weight, preferred_element_type=F32)
    activated, pullback = jax.vjp(smooth, pre_act)
    hidden = activated.astype(BF)
    out_part = jnp.einsum("erf,efd->erd", hidden, out_weight, preferred_element_type=F32).astype(BF)
    hidden_grad = jnp.einsum("erd,efd->erf", got_grads, out_weight, preferred_element_type=F32)
    pre_grad = pullback(hidden_grad)[0].astype(BF)
    slot_part = jnp.einsum("erf,edf->erd", pre_grad, in_weight, preferred_element_type=F32).astype(BF)
    parts = jnp.concatenate([out_part.reshape(128, width), slot_part.reshape(128, width)])
    to, core_of = row // 16, (row // 8) % 2
    source = (mirror * (1 - 2 * core_of) * to) % 16
    order = (row // 2) % 4 * 64 + source * 4 + core_of * 2 + row % 2
    scattered = lax.all_to_all(picked(order, parts).reshape(16, 16, width), PLANE, 0, 0, tiled=True)
    summed = jnp.sum(scattered.astype(F32), axis=0).astype(BF)
    near, far = shifted(summed, -1), shifted(summed, -1, 16)
    out_weight_grad = jnp.einsum("erf,erd->efd", hidden, got_grads, preferred_element_type=F32).astype(BF)
    in_weight_grad = jnp.einsum("erd,erf->edf", got_slots, pre_grad, preferred_element_type=F32).astype(BF)
    home = (near.astype(F32) + far.astype(F32)).astype(BF)
    back = spread(home.reshape(2, 8, width)).reshape(256, width)
    expert = row % 64
    core_of = (expert // 2) % 2
    source = ((1 - 2 * core_of) * (expert // 4 - z_lo)) % 16
    order = source * 16 + core_of * 8 + row // 128 * 4 + expert % 2 * 2 + (row // 64) % 2
    results = picked(order, back).reshape(2, 2, 64, width)
    expert_out, slot_grad = results[0], results[1]
    combine_grad = jnp.einsum("itd,ied->ite", out_grad, expert_out, preferred_element_type=F32)
    dispatch_grad = jnp.einsum("itd,ied->ite", tokens, slot_grad, preferred_element_type=F32)
    from_dispatch = dispatch * (dispatch_grad - jnp.sum(dispatch * dispatch_grad, axis=1, keepdims=True))
    from_combine = combine * (combine_grad - jnp.sum(combine * combine_grad, axis=2, keepdims=True))
    logit_grad = (from_dispatch + from_combine).astype(BF)
    local_proj = jnp.einsum("itd,ite->de", tokens, logit_grad, preferred_element_type=F32)
    share = width // 16
    mine = lax.dynamic_slice_in_dim(local_proj, column * share, share, 0).astype(BF)
    mine = jnp.sum(gathered(mine, ("zr", "c"), 8).astype(F32), axis=0).astype(BF)
    mine = jnp.sum(gathered(mine, "zq", 4).astype(F32), axis=0).astype(BF)
    proj_grad = gathered(mine, PLANE, 16).reshape(width, 64)
    mixed = jnp.einsum("ite,ied->itd", combine_b, expert_out, preferred_element_type=F32).astype(BF)
    token_grad = (
        jnp.einsum("ite,ied->itd", dispatch_b, slot_grad, preferred_element_type=F32)
        + jnp.einsum("ite,de->itd", logit_grad, slot_proj, preferred_element_type=F32)
    ).astype(BF)
    return (mixed, token_grad, proj_grad, in_weight_grad, out_weight_grad)


def solution(mesh):
    fine = Mesh(mesh.devices.reshape(4, 2, 4, 4, 4, 2), ALL)
    images, first, second = P(EXP, None, None), P(EXP, None, REP), P(EXP, REP, None)
    return jax.shard_map(
        on_device,
        mesh=fine,
        in_specs=(images, P(), first, second, images),
        out_specs=(images, images, P(), first, second),
        check_vma=False,
    )
```

```python
import jax
import jax.numpy as jnp
from jax import lax
from jax.sharding import Mesh, PartitionSpec as P

ALL = ("y", "zh", "x", "zq", "zr", "c")
PLANE = ("y", "x")
EXP = ("zq", "zr", "c")
REP = ("y", "zh", "x")
BF = jnp.bfloat16
F32 = jnp.float32


def signed(r):
    return r if r <= 8 else r - 16


def shifted(value, shift):
    pairs = []
    for y in range(4):
        for x in range(4):
            for z in range(32):
                for c in range(2):
                    to = (z + shift(y, x, c)) % 32
                    source = (((y * 2 + z // 16) * 4 + x) * 16 + z % 16) * 2 + c
                    target = (((y * 2 + to // 16) * 4 + x) * 16 + to % 16) * 2 + c
                    pairs.append((source, target))
    return lax.ppermute(value, ALL, pairs)


def out_shift(y, x, c):
    return signed(4 * y + x) * (1 - 2 * c)


def swapped(rows):
    return jnp.concatenate([rows[:1], lax.ppermute(rows[1:], "c", [(0, 1), (1, 0)])])


def smooth(values):
    return jax.nn.gelu(values, approximate=True)


def picked(index, rows):
    choose = (index[:, None] == jnp.arange(rows.shape[0])[None, :]).astype(BF)
    return jnp.dot(choose, rows, preferred_element_type=F32).astype(BF)


def gathered(value, axes, size):
    out = jnp.broadcast_to(value[None], (size,) + value.shape)
    return lax.all_to_all(out, axes, 0, 0, tiled=True)


def on_device(tokens, slot_proj, in_weight, out_weight, out_grad):
    width = tokens.shape[2]
    column = lax.axis_index("y") * 4 + lax.axis_index("x")
    core = lax.axis_index("c")
    z_lo = lax.axis_index("zq") * 4 + lax.axis_index("zr")
    logits = jnp.einsum("itd,de->ite", tokens, slot_proj, preferred_element_type=F32)
    dispatch = jax.nn.softmax(logits, axis=1)
    combine = jax.nn.softmax(logits, axis=2)
    dispatch_b = dispatch.astype(BF)
    combine_b = combine.astype(BF)
    slot_rows = jnp.einsum("ite,itd->ied", dispatch_b, tokens, preferred_element_type=F32).astype(BF)
    expert_grad = jnp.einsum("ite,itd->ied", combine_b, out_grad, preferred_element_type=F32).astype(BF)
    both = jnp.concatenate([slot_rows.reshape(128, width), expert_grad.reshape(128, width)])
    row = jnp.arange(16)
    to_core = core ^ (row // 8)
    target = (z_lo + (1 - 2 * to_core) * column) % 16
    wanted = (row // 4) % 2 * 128 + row % 2 * 64 + 4 * target + 2 * to_core + (row // 2) % 2
    held = swapped(picked(wanted, both).reshape(2, 8, width))
    sent = shifted(held.reshape(16, width), out_shift)
    got = gathered(sent, PLANE, 16).reshape(256, width)
    row = jnp.arange(256)
    order = (row // 2) % 32 * 8 + row // 64 * 2 + row % 2
    kinds = picked(order, got).reshape(2, 2, 64, width)
    got_slots, got_grads = kinds[0], kinds[1]
    pre_act = jnp.einsum("erd,edf->erf", got_slots, in_weight, preferred_element_type=F32)
    activated, pullback = jax.vjp(smooth, pre_act)
    hidden = activated.astype(BF)
    out_part = jnp.einsum("erf,efd->erd", hidden, out_weight, preferred_element_type=F32).astype(BF)
    hidden_grad = jnp.einsum("erd,efd->erf", got_grads, out_weight, preferred_element_type=F32)
    pre_grad = pullback(hidden_grad)[0].astype(BF)
    slot_part = jnp.einsum("erf,edf->erd", pre_grad, in_weight, preferred_element_type=F32).astype(BF)
    parts = jnp.concatenate([out_part.reshape(128, width), slot_part.reshape(128, width)])
    order = (row // 2) % 4 * 64 + row // 16 * 4 + (row // 8) % 2 * 2 + row % 2
    scattered = lax.all_to_all(picked(order, parts).reshape(16, 16, width), PLANE, 0, 0, tiled=True)
    summed = jnp.sum(scattered.astype(F32), axis=0).astype(BF)
    far = shifted(summed, lambda y, x, c: 16 - out_shift(y, x, c))
    near = shifted(summed, lambda y, x, c: -out_shift(y, x, c))
    out_weight_grad = jnp.einsum("erf,erd->efd", hidden, got_grads, preferred_element_type=F32).astype(BF)
    in_weight_grad = jnp.einsum("erd,erf->edf", got_slots, pre_grad, preferred_element_type=F32).astype(BF)
    home = (near.astype(F32) + far.astype(F32)).astype(BF)
    back = gathered(swapped(home.reshape(2, 8, width)).reshape(16, width), PLANE, 16).reshape(256, width)
    expert = row % 64
    core_of = (expert // 2) % 2
    source = ((1 - 2 * core_of) * (expert // 4 - z_lo)) % 16
    order = source * 16 + (core_of ^ core) * 8 + row // 128 * 4 + expert % 2 * 2 + (row // 64) % 2
    results = picked(order, back).reshape(2, 2, 64, width)
    expert_out, slot_grad = results[0], results[1]
    combine_grad = jnp.einsum("itd,ied->ite", out_grad, expert_out, preferred_element_type=F32)
    dispatch_grad = jnp.einsum("itd,ied->ite", tokens, slot_grad, preferred_element_type=F32)
    from_dispatch = dispatch * (dispatch_grad - jnp.sum(dispatch * dispatch_grad, axis=1, keepdims=True))
    from_combine = combine * (combine_grad - jnp.sum(combine * combine_grad, axis=2, keepdims=True))
    logit_grad = (from_dispatch + from_combine).astype(BF)
    half = width // 2
    local_proj = jnp.concatenate(
        [jnp.einsum("itd,ite->de", part, logit_grad, preferred_element_type=F32)
         for part in (tokens[:, :, :half], tokens[:, :, half:])], axis=1)
    share = half // 4
    mine = lax.dynamic_slice_in_dim(local_proj, lax.axis_index("y") * share, share, 0).astype(BF)
    mine = jnp.sum(gathered(mine, ("zr", "c"), 8).astype(F32), axis=0).astype(BF)
    mine = shifted(mine, lambda y, x, c: 4 * (0, 1, 2, -1)[x])
    shares = gathered(mine, PLANE, 16).reshape(4, 4, share, 128)
    sums = jnp.sum(shares.astype(F32), axis=1).astype(BF).reshape(half, 128)
    proj_grad = jnp.concatenate([sums[:, :64], sums[:, 64:]], axis=0)
    mixed = jnp.einsum("ite,ied->itd", combine_b, expert_out, preferred_element_type=F32).astype(BF)
    token_grad = (
        jnp.einsum("ite,ied->itd", dispatch_b, slot_grad, preferred_element_type=F32)
        + jnp.einsum("ite,de->itd", logit_grad, slot_proj, preferred_element_type=F32)
    ).astype(BF)
    return (mixed, token_grad, proj_grad, in_weight_grad, out_weight_grad)


def solution(mesh):
    fine = Mesh(mesh.devices.reshape(4, 2, 4, 4, 4, 2), ALL)
    images, first, second = P(EXP, None, None), P(EXP, None, REP), P(EXP, REP, None)
    return jax.shard_map(
        on_device,
        mesh=fine,
        in_specs=(images, P(), first, second, images),
        out_specs=(images, images, P(), first, second),
        check_vma=False,
    )
```

```python
import jax
import jax.numpy as jnp
import numpy as np
from jax import lax
from jax.sharding import Mesh, PartitionSpec as P

ALL = ("y", "zh", "x", "zq", "zr", "c")
PLANE = ("y", "x")
EXP = ("zq", "zr", "c")
REP = ("y", "zh", "x")
BF = jnp.bfloat16
F32 = jnp.float32


def signed(r):
    return r if r <= 8 else r - 16


def shifted(value, shift):
    pairs = []
    for y in range(4):
        for x in range(4):
            for z in range(32):
                for c in range(2):
                    to = (z + shift(y, x, c)) % 32
                    source = (((y * 2 + z // 16) * 4 + x) * 16 + z % 16) * 2 + c
                    target = (((y * 2 + to // 16) * 4 + x) * 16 + to % 16) * 2 + c
                    pairs.append((source, target))
    return lax.ppermute(value, ALL, pairs)


def out_shift(y, x, c):
    return signed(4 * y + x) * (1 - 2 * c)


def swapped(rows):
    return jnp.concatenate([rows[:1], lax.ppermute(rows[1:], "c", [(0, 1), (1, 0)])])


def smooth(values):
    return jax.nn.gelu(values, approximate=True)


def chooser(index, size):
    return (index[:, None] == jnp.arange(size)[None, :]).astype(BF)


def chosen(index, size):
    return jnp.asarray((index[:, None] == np.arange(size)[None, :]).astype(BF))


def picked(choose, rows):
    return jnp.dot(choose, rows, preferred_element_type=F32).astype(BF)


def added(rows, groups, inner):
    to, source = np.arange(groups * inner), np.arange(rows.shape[0])
    span = rows.shape[0] // groups
    same = (source[None, :] // span == to[:, None] // inner) & (source[None, :] % inner == to[:, None] % inner)
    return jnp.dot(jnp.asarray(same.astype(BF)), rows, preferred_element_type=F32).astype(BF)


def tied(*values):
    return lax.optimization_barrier(values)


def gathered(value, axes, size):
    out = jnp.broadcast_to(value[None], (size,) + value.shape)
    return lax.all_to_all(out, axes, 0, 0, tiled=True)


def on_device(tokens, slot_proj, in_weight, out_weight, out_grad):
    width = tokens.shape[2]
    column = lax.axis_index("y") * 4 + lax.axis_index("x")
    core = lax.axis_index("c")
    z_lo = lax.axis_index("zq") * 4 + lax.axis_index("zr")
    row = jnp.arange(16)
    to_core = core ^ (row // 8)
    target = (z_lo + (1 - 2 * to_core) * column) % 16
    outgoing = chooser((row // 4) % 2 * 128 + row % 2 * 64 + 4 * target + 2 * to_core + (row // 2) % 2, 256)
    static, row = np.arange(256), jnp.arange(256)
    by_expert = chosen((static // 2) % 32 * 8 + static // 64 * 2 + static % 2, 256)
    by_column = chosen((static // 2) % 4 * 64 + static // 16 * 4 + (static // 8) % 2 * 2 + static % 2, 256)
    expert = row % 64
    core_of = (expert // 2) % 2
    source = ((1 - 2 * core_of) * (expert // 4 - z_lo)) % 16
    by_image = chooser(
        source * 16 + (core_of ^ core) * 8 + row // 128 * 4 + expert % 2 * 2 + (row // 64) % 2, 256
    )

    logits = jnp.einsum("itd,de->ite", tokens, slot_proj, preferred_element_type=F32)
    dispatch = jax.nn.softmax(logits, axis=1)
    combine = jax.nn.softmax(logits, axis=2)
    dispatch_b = dispatch.astype(BF)
    combine_b = combine.astype(BF)
    slot_rows = jnp.einsum("ite,itd->ied", dispatch_b, tokens, preferred_element_type=F32).astype(BF)
    expert_grad = jnp.einsum("ite,itd->ied", combine_b, out_grad, preferred_element_type=F32).astype(BF)
    both = jnp.concatenate([slot_rows.reshape(128, width), expert_grad.reshape(128, width)])
    held = swapped(picked(outgoing, both).reshape(2, 8, width))
    sent = shifted(held.reshape(16, width), out_shift)
    sent, by_image, first = tied(sent, by_image, lax.axis_index("y") * 16)
    got = gathered(sent, PLANE, 16).reshape(256, width)
    kinds = picked(by_expert, got).reshape(2, 2, 64, width)
    got_slots, got_grads = kinds[0], kinds[1]
    pre_act = jnp.einsum("erd,edf->erf", got_slots, in_weight, preferred_element_type=F32)
    activated, pullback = jax.vjp(smooth, pre_act)
    hidden = activated.astype(BF)
    out_part = jnp.einsum("erf,efd->erd", hidden, out_weight, preferred_element_type=F32).astype(BF)
    hidden_grad = jnp.einsum("erd,efd->erf", got_grads, out_weight, preferred_element_type=F32)
    pre_grad = pullback(hidden_grad)[0].astype(BF)
    slot_part = jnp.einsum("erf,edf->erd", pre_grad, in_weight, preferred_element_type=F32).astype(BF)
    parts = jnp.concatenate([out_part.reshape(128, width), slot_part.reshape(128, width)])
    scattered = lax.all_to_all(picked(by_column, parts).reshape(16, 16, width), PLANE, 0, 0, tiled=True)
    summed = added(scattered.reshape(256, width), 1, 16)
    summed, hidden, pre_grad, got_slots, got_grads = tied(summed, hidden, pre_grad, got_slots, got_grads)
    near = shifted(summed, lambda y, x, c: -out_shift(y, x, c))
    far = shifted(summed, lambda y, x, c: 16 - out_shift(y, x, c))
    out_weight_grad = jnp.einsum("erf,erd->efd", hidden, got_grads, preferred_element_type=F32).astype(BF)
    in_weight_grad = jnp.einsum("erd,erf->edf", got_slots, pre_grad, preferred_element_type=F32).astype(BF)
    near, far, out_weight_grad, in_weight_grad = tied(near, far, out_weight_grad, in_weight_grad)
    home = (near.astype(F32) + far.astype(F32)).astype(BF)
    back = gathered(swapped(home.reshape(2, 8, width)).reshape(16, width), PLANE, 16).reshape(256, width)
    results = picked(by_image, back).reshape(2, 2, 64, width)
    expert_out, slot_grad = results[0], results[1]
    combine_grad = jnp.einsum("itd,ied->ite", out_grad, expert_out, preferred_element_type=F32)
    dispatch_grad = jnp.einsum("itd,ied->ite", tokens, slot_grad, preferred_element_type=F32)
    from_dispatch = dispatch * (dispatch_grad - jnp.sum(dispatch * dispatch_grad, axis=1, keepdims=True))
    from_combine = combine * (combine_grad - jnp.sum(combine * combine_grad, axis=2, keepdims=True))
    logit_grad = (from_dispatch + from_combine).astype(BF)
    own = lax.dynamic_slice(logit_grad, (0, 0, first), (2, 256, 16), allow_negative_indices=False)
    mine = jnp.einsum("ite,itd->ed", own, tokens, preferred_element_type=F32).astype(BF)
    mine = added(gathered(mine, ("zr", "c"), 8).reshape(128, width), 1, 16)
    mine, logit_grad, expert_out, slot_grad = tied(mine, logit_grad, expert_out, slot_grad)
    mine = shifted(mine, lambda y, x, c: 4 * (0, 1, 2, -1)[x])
    mixed = jnp.einsum("ite,ied->itd", combine_b, expert_out, preferred_element_type=F32).astype(BF)
    weights = jnp.concatenate([dispatch_b, logit_grad], axis=2)
    vectors = jnp.concatenate([slot_grad, jnp.broadcast_to(slot_proj.T, (2, 64, width))], axis=1)
    token_grad = jnp.einsum("itk,ikd->itd", weights, vectors, preferred_element_type=F32).astype(BF)
    mine, mixed, token_grad = tied(mine, mixed, token_grad)
    shares = gathered(mine, PLANE, 16).reshape(256, width)
    proj_grad = added(shares, 4, 16).T
    return (mixed, token_grad, proj_grad, in_weight_grad, out_weight_grad)


def solution(mesh):
    fine = Mesh(mesh.devices.reshape(4, 2, 4, 4, 4, 2), ALL)
    images, first, second = P(EXP, None, None), P(EXP, None, REP), P(EXP, REP, None)
    return jax.shard_map(
        on_device,
        mesh=fine,
        in_specs=(images, P(), first, second, images),
        out_specs=(images, images, P(), first, second),
        check_vma=False,
    )
```

```python
import jax
import jax.numpy as jnp
import numpy as np
from jax import lax
from jax.experimental import pallas as pl
from jax.experimental.pallas import tpu as pltpu
from jax.sharding import Mesh, PartitionSpec as P

ALL = ("y", "zh", "x", "zq", "zr", "c")
PLANE = ("y", "x")
EXP = ("zq", "zr", "c")
REP = ("y", "zh", "x")
BF = jnp.bfloat16
F32 = jnp.float32


def signed(r):
    return r if r <= 8 else r - 16


def shifted(value, shift):
    pairs = []
    for y in range(4):
        for x in range(4):
            for z in range(32):
                for c in range(2):
                    to = (z + shift(y, x, c)) % 32
                    source = (((y * 2 + z // 16) * 4 + x) * 16 + z % 16) * 2 + c
                    target = (((y * 2 + to // 16) * 4 + x) * 16 + to % 16) * 2 + c
                    pairs.append((source, target))
    return lax.ppermute(value, ALL, pairs)


def out_shift(y, x, c):
    return signed(4 * y + x) * (1 - 2 * c)


def swapped(rows):
    return jnp.concatenate([rows[:1], lax.ppermute(rows[1:], "c", [(0, 1), (1, 0)])])


def smooth(values):
    return jax.nn.gelu(values, approximate=True)


def chooser(index, size):
    return (index[:, None] == jnp.arange(size)[None, :]).astype(BF)


def chosen(index, size):
    return jnp.asarray((index[:, None] == np.arange(size)[None, :]).astype(BF))


def picked(choose, rows):
    return jnp.dot(choose, rows, preferred_element_type=F32).astype(BF)


def added(rows, groups, inner):
    to, source = np.arange(groups * inner), np.arange(rows.shape[0])
    span = rows.shape[0] // groups
    same = (source[None, :] // span == to[:, None] // inner) & (source[None, :] % inner == to[:, None] % inner)
    return jnp.dot(jnp.asarray(same.astype(BF)), rows, preferred_element_type=F32).astype(BF)


def tied(*values):
    return lax.optimization_barrier(values)


def gathered(value, axes, size):
    out = jnp.broadcast_to(value[None], (size,) + value.shape)
    return lax.all_to_all(out, axes, 0, 0, tiled=True)


def front_body(place_ref, tokens_ref, cotangent_ref, proj_ref, sent_ref, dispatch_ref, combine_ref, rows_ref):
    image = pl.program_id(0)
    tokens = tokens_ref[0]
    logits = lax.dot_general(proj_ref[...], tokens, (((1,), (1,)), ((), ())), preferred_element_type=F32)
    raised = jnp.exp(logits - jnp.max(logits, axis=1, keepdims=True))
    dispatch = raised / jnp.sum(raised, axis=1, keepdims=True)
    raised = jnp.exp(logits - jnp.max(logits, axis=0, keepdims=True))
    combine = raised / jnp.sum(raised, axis=0, keepdims=True)
    dispatch_ref[0] = dispatch
    combine_ref[0] = combine
    first = pl.multiple_of(image * 64, 64)
    rows_ref[pl.ds(first, 64), :] = jnp.dot(dispatch.astype(BF), tokens, preferred_element_type=F32).astype(BF)
    rows_ref[pl.ds(first + 128, 64), :] = jnp.dot(
        combine.astype(BF), cotangent_ref[0], preferred_element_type=F32
    ).astype(BF)

    @pl.when(image == 1)
    def _():
        z_lo, column, core = place_ref[0], place_ref[1], place_ref[2]
        row = lax.broadcasted_iota(jnp.int32, (16, 256), 0)
        near = (z_lo + (1 - 2 * core) * column) & 15
        cross = (z_lo - (1 - 2 * core) * column) & 15
        block = jnp.where(row < 8, 4 * near + 2 * core, 4 * cross + 2 * (1 - core))
        wanted = ((row >> 2) & 1) * 128 + (row & 1) * 64 + block + ((row >> 1) & 1)
        choose = (wanted == lax.broadcasted_iota(jnp.int32, (16, 256), 1)).astype(F32).astype(BF)
        sent_ref[...] = jnp.dot(choose, rows_ref[...], preferred_element_type=F32).astype(BF)


def front(place, tokens, cotangent, proj):
    width = tokens.shape[2]
    image = pl.BlockSpec((1, 256, width), lambda i: (i, 0, 0))
    scores = pl.BlockSpec((1, 64, 256), lambda i: (i, 0, 0))
    return pl.pallas_call(
        front_body,
        grid=(2,),
        in_specs=[pl.BlockSpec(memory_space=pltpu.SMEM), image, image, pl.BlockSpec((64, width), lambda i: (0, 0))],
        out_specs=[pl.BlockSpec((16, width), lambda i: (0, 0)), scores, scores],
        out_shape=[
            jax.ShapeDtypeStruct((16, width), BF),
            jax.ShapeDtypeStruct((2, 64, 256), F32),
            jax.ShapeDtypeStruct((2, 64, 256), F32),
        ],
        scratch_shapes=[pltpu.VMEM((256, width), BF)],
        compiler_params=pltpu.CompilerParams(vmem_limit_bytes=56 * 2**20),
    )(place, tokens, cotangent, proj)


def on_device(tokens, slot_proj, in_weight, out_weight, out_grad):
    width = tokens.shape[2]
    column = lax.axis_index("y") * 4 + lax.axis_index("x")
    core = lax.axis_index("c")
    z_lo = lax.axis_index("zq") * 4 + lax.axis_index("zr")
    static, row = np.arange(256), jnp.arange(256)
    by_expert = chosen((static // 2) % 32 * 8 + static // 64 * 2 + static % 2, 256)
    by_column = chosen((static // 2) % 4 * 64 + static // 16 * 4 + (static // 8) % 2 * 2 + static % 2, 256)
    expert = row % 64
    core_of = (expert // 2) % 2
    source = ((1 - 2 * core_of) * (expert // 4 - z_lo)) % 16
    by_image = chooser(
        source * 16 + core_of * 8 + row // 128 * 4 + expert % 2 * 2 + (row // 64) % 2, 256
    )

    place = jnp.stack([z_lo, column, core]).astype(jnp.int32)
    outgoing, dispatch, combine = front(place, tokens, out_grad, slot_proj.T)
    dispatch, combine = jnp.swapaxes(dispatch, 1, 2), jnp.swapaxes(combine, 1, 2)
    dispatch_b, combine_b = dispatch.astype(BF), combine.astype(BF)
    held = swapped(outgoing.reshape(2, 8, width))
    sent = shifted(held.reshape(16, width), out_shift)
    sent, by_image, first, dispatch_b, combine_b, leading = tied(
        sent, by_image, lax.axis_index("y") * 16, dispatch_b, combine_b, core == 0
    )
    got = gathered(sent, PLANE, 16).reshape(256, width)
    kinds = picked(by_expert, got).reshape(2, 2, 64, width)
    got_slots, got_grads = kinds[0], kinds[1]
    pre_act = jnp.einsum("erd,edf->erf", got_slots, in_weight, preferred_element_type=F32)
    activated, pullback = jax.vjp(smooth, pre_act)
    hidden = activated.astype(BF)
    out_part = jnp.einsum("erf,efd->erd", hidden, out_weight, preferred_element_type=F32).astype(BF)
    hidden_grad = jnp.einsum("erd,efd->erf", got_grads, out_weight, preferred_element_type=F32)
    pre_grad = pullback(hidden_grad)[0].astype(BF)
    slot_part = jnp.einsum("erf,edf->erd", pre_grad, in_weight, preferred_element_type=F32).astype(BF)
    parts = jnp.concatenate([out_part.reshape(128, width), slot_part.reshape(128, width)])
    scattered = lax.all_to_all(picked(by_column, parts).reshape(16, 16, width), PLANE, 0, 0, tiled=True)
    summed = added(scattered.reshape(256, width), 1, 16)
    summed, hidden, pre_grad, got_slots, got_grads = tied(summed, hidden, pre_grad, got_slots, got_grads)
    near = shifted(summed, lambda y, x, c: -out_shift(y, x, c))
    far = shifted(summed, lambda y, x, c: 16 - out_shift(y, x, c))
    out_weight_grad = jnp.einsum("erf,erd->efd", hidden, got_grads, preferred_element_type=F32).astype(BF)
    in_weight_grad = jnp.einsum("erd,erf->edf", got_slots, pre_grad, preferred_element_type=F32).astype(BF)
    near, far, out_weight_grad, in_weight_grad = tied(near, far, out_weight_grad, in_weight_grad)
    home = (near.astype(F32) + far.astype(F32)).astype(BF)
    mine = home.reshape(2, 8, width)
    mine = jnp.broadcast_to(jnp.where(leading, mine, mine[::-1])[None], (16, 2, 8, width))
    back = lax.all_to_all(mine.reshape(32, 8, width), PLANE + ("c",), 0, 0, tiled=True).reshape(256, width)
    results = picked(by_image, back).reshape(2, 2, 64, width)
    expert_out, slot_grad = results[0], results[1]
    combine_grad = jnp.einsum("itd,ied->ite", out_grad, expert_out, preferred_element_type=F32)
    dispatch_grad = jnp.einsum("itd,ied->ite", tokens, slot_grad, preferred_element_type=F32)
    from_dispatch = dispatch * (dispatch_grad - jnp.sum(dispatch * dispatch_grad, axis=1, keepdims=True))
    from_combine = combine * (combine_grad - jnp.sum(combine * combine_grad, axis=2, keepdims=True))
    logit_grad = (from_dispatch + from_combine).astype(BF)
    own = lax.dynamic_slice(logit_grad, (0, 0, first), (2, 256, 16), allow_negative_indices=False)
    mine = jnp.einsum("ite,itd->ed", own, tokens, preferred_element_type=F32).astype(BF)
    mixed = jnp.einsum("ite,ied->itd", combine_b, expert_out, preferred_element_type=F32).astype(BF)
    mine = added(gathered(mine, ("zr", "c"), 8).reshape(128, width), 1, 16)
    mine, mixed, logit_grad, slot_grad = tied(mine, mixed, logit_grad, slot_grad)
    mine = shifted(mine, lambda y, x, c: 4 * (0, 1, 2, -1)[x])
    weights = jnp.concatenate([dispatch_b, logit_grad], axis=2)
    vectors = jnp.concatenate([slot_grad, jnp.broadcast_to(slot_proj.T, (2, 64, width))], axis=1)
    token_grad = jnp.einsum("itk,ikd->itd", weights, vectors, preferred_element_type=F32).astype(BF)
    mine, token_grad = tied(mine, token_grad)
    shares = gathered(mine, PLANE, 16).reshape(256, width)
    proj_grad = added(shares, 4, 16).T
    return (mixed, token_grad, proj_grad, in_weight_grad, out_weight_grad)


def solution(mesh):
    fine = Mesh(mesh.devices.reshape(4, 2, 4, 4, 4, 2), ALL)
    images, first, second = P(EXP, None, None), P(EXP, None, REP), P(EXP, REP, None)
    return jax.shard_map(
        on_device,
        mesh=fine,
        in_specs=(images, P(), first, second, images),
        out_specs=(images, images, P(), first, second),
        check_vma=False,
    )
```

```python
import jax
import jax.numpy as jnp
import numpy as np
from jax import lax
from jax.experimental import pallas as pl
from jax.experimental.pallas import tpu as pltpu
from jax.sharding import Mesh, PartitionSpec as P

ALL = ("y", "zh", "x", "zq", "zr", "c")
PLANE = ("y", "x")
EXP = ("zq", "zr", "c")
REP = ("y", "zh", "x")
BF = jnp.bfloat16
F32 = jnp.float32


def signed(r):
    return r if r <= 8 else r - 16


def shifted(value, shift):
    pairs = []
    for y in range(4):
        for x in range(4):
            for z in range(32):
                for c in range(2):
                    to = (z + shift(y, x, c)) % 32
                    source = (((y * 2 + z // 16) * 4 + x) * 16 + z % 16) * 2 + c
                    target = (((y * 2 + to // 16) * 4 + x) * 16 + to % 16) * 2 + c
                    pairs.append((source, target))
    return lax.ppermute(value, ALL, pairs)


def out_shift(y, x, c):
    return signed(4 * y + x) * (1 - 2 * c)


def spread(rows):
    out = jnp.broadcast_to(rows[None], (16,) + rows.shape).reshape((32,) + rows.shape[1:])
    return lax.all_to_all(out, PLANE + ("c",), 0, 0, tiled=True)


def chooser(index, size):
    return (index[:, None] == jnp.arange(size)[None, :]).astype(BF)


def picked(choose, rows):
    return jnp.dot(choose, rows, preferred_element_type=F32).astype(BF)


def added(rows, groups, inner):
    to, source = np.arange(groups * inner), np.arange(rows.shape[0])
    span = rows.shape[0] // groups
    same = (source[None, :] // span == to[:, None] // inner) & (source[None, :] % inner == to[:, None] % inner)
    return jnp.dot(jnp.asarray(same.astype(BF)), rows, preferred_element_type=F32).astype(BF)


def tied(*values):
    return lax.optimization_barrier(values)


def gathered(value, axes, size):
    out = jnp.broadcast_to(value[None], (size,) + value.shape)
    return lax.all_to_all(out, axes, 0, 0, tiled=True)


def front_body(place_ref, tokens_ref, cotangent_ref, proj_ref, sent_ref, dispatch_ref, combine_ref, rows_ref):
    for image in range(2):
        tokens = tokens_ref[image]
        logits = lax.dot_general(proj_ref[...], tokens, (((1,), (1,)), ((), ())), preferred_element_type=F32)
        raised = jnp.exp(logits - jnp.max(logits, axis=1, keepdims=True))
        dispatch = raised / jnp.sum(raised, axis=1, keepdims=True)
        raised = jnp.exp(logits - jnp.max(logits, axis=0, keepdims=True))
        combine = raised / jnp.sum(raised, axis=0, keepdims=True)
        dispatch_ref[image] = dispatch
        combine_ref[image] = combine
        rows_ref[64 * image : 64 * image + 64, :] = jnp.dot(
            dispatch.astype(BF), tokens, preferred_element_type=F32
        ).astype(BF)
        rows_ref[64 * image + 128 : 64 * image + 192, :] = jnp.dot(
            combine.astype(BF), cotangent_ref[image], preferred_element_type=F32
        ).astype(BF)
    z_lo, column, core = place_ref[0], place_ref[1], place_ref[2]
    row = lax.broadcasted_iota(jnp.int32, (16, 256), 0)
    target = (z_lo + (1 - 2 * core) * column) & 15
    wanted = ((row >> 2) & 1) * 128 + (row & 1) * 64 + 4 * target + (row >> 3) * 2 + ((row >> 1) & 1)
    choose = (wanted == lax.broadcasted_iota(jnp.int32, (16, 256), 1)).astype(F32).astype(BF)
    sent_ref[...] = jnp.dot(choose, rows_ref[...], preferred_element_type=F32).astype(BF)


def front(place, tokens, cotangent, proj):
    width = tokens.shape[2]
    vmem = pl.BlockSpec(memory_space=pltpu.VMEM)
    return pl.pallas_call(
        front_body,
        in_specs=[pl.BlockSpec(memory_space=pltpu.SMEM), vmem, vmem, vmem],
        out_specs=[vmem, vmem, vmem],
        out_shape=[
            jax.ShapeDtypeStruct((16, width), BF),
            jax.ShapeDtypeStruct((2, 64, 256), F32),
            jax.ShapeDtypeStruct((2, 64, 256), F32),
        ],
        scratch_shapes=[pltpu.VMEM((256, width), BF)],
        compiler_params=pltpu.CompilerParams(vmem_limit_bytes=56 * 2**20),
    )(place, tokens, cotangent, proj)


def experts_body(place_ref, got_ref, first_ref, second_ref, out_ref, rows_ref, hidden_ref, grad_ref, parts_ref):
    which = pl.program_id(0)
    row = lax.broadcasted_iota(jnp.int32, (128, 256), 0)
    wanted = ((row >> 1) & 31) * 8 + (row >> 6) * 4 + which * 2 + (row & 1)
    choose = (wanted == lax.broadcasted_iota(jnp.int32, (128, 256), 1)).astype(F32).astype(BF)
    rows = jnp.dot(choose, got_ref[...], preferred_element_type=F32).astype(BF)
    rows_ref[0] = rows
    slots, cotangents = rows[:64], rows[64:]
    first, second = first_ref[0], second_ref[0]
    turned = (((1,), (1,)), ((), ()))
    v = lax.dot_general(slots, first, turned, preferred_element_type=F32)
    hidden_grad = lax.dot_general(cotangents, second, turned, preferred_element_type=F32)
    root = 0.7978845608028654
    square = v * v
    t = jnp.tanh(root * v * (1.0 + 0.044715 * square))
    hidden = (0.5 * v * (1.0 + t)).astype(BF)
    slope = 0.5 * (1.0 + t) + 0.5 * v * (1.0 - t * t) * (root * (1.0 + 3.0 * 0.044715 * square))
    pre_grad = (hidden_grad * slope).astype(BF)
    hidden_ref[0] = hidden
    grad_ref[0] = pre_grad
    start = pl.multiple_of(which * 128, 128)
    parts_ref[pl.ds(start, 64), :] = jnp.dot(hidden, second, preferred_element_type=F32).astype(BF)
    parts_ref[pl.ds(start + 64, 64), :] = jnp.dot(pre_grad, first, preferred_element_type=F32).astype(BF)

    @pl.when(which == 1)
    def _():
        core = place_ref[2]
        row = lax.broadcasted_iota(jnp.int32, (256, 256), 0)
        other = (row >> 3) & 1
        to = row >> 4
        source = jnp.where(other == 1, (16 - to) & 15, to)
        image_core = jnp.where(other == 1, 1 - core, core)
        wanted = ((row >> 1) & 1) * 128 + ((row >> 2) & 1) * 64 + source * 4 + image_core * 2 + (row & 1)
        choose = (wanted == lax.broadcasted_iota(jnp.int32, (256, 256), 1)).astype(F32).astype(BF)
        out_ref[...] = jnp.dot(choose, parts_ref[...], preferred_element_type=F32).astype(BF)


def experts(place, got, first, second):
    width = got.shape[1]
    units = first.shape[1]
    whole = pl.BlockSpec((256, width), lambda i: (0, 0))
    weight = pl.BlockSpec((1, units, width), lambda i: (i, 0, 0))
    act = pl.BlockSpec((1, 64, units), lambda i: (i, 0, 0))
    return pl.pallas_call(
        experts_body,
        grid=(2,),
        in_specs=[pl.BlockSpec(memory_space=pltpu.SMEM), whole, weight, weight],
        out_specs=[whole, pl.BlockSpec((1, 128, width), lambda i: (i, 0, 0)), act, act],
        out_shape=[
            jax.ShapeDtypeStruct((256, width), BF),
            jax.ShapeDtypeStruct((2, 128, width), BF),
            jax.ShapeDtypeStruct((2, 64, units), BF),
            jax.ShapeDtypeStruct((2, 64, units), BF),
        ],
        scratch_shapes=[pltpu.VMEM((256, width), BF)],
        compiler_params=pltpu.CompilerParams(vmem_limit_bytes=24 * 2**20),
    )(place, got, first, second)


def on_device(tokens, slot_proj, in_weight, out_weight, out_grad):
    width = tokens.shape[2]
    column = lax.axis_index("y") * 4 + lax.axis_index("x")
    core = lax.axis_index("c")
    z_lo = lax.axis_index("zq") * 4 + lax.axis_index("zr")
    row = jnp.arange(256)
    expert = row % 64
    core_of = (expert // 2) % 2
    source = ((1 - 2 * core_of) * (expert // 4 - z_lo)) % 16
    by_image = chooser(
        source * 16 + core_of * 8 + row // 128 * 4 + expert % 2 * 2 + (row // 64) % 2, 256
    )

    place = jnp.stack([z_lo, column, core]).astype(jnp.int32)
    outgoing, dispatch, combine = front(place, tokens, out_grad, slot_proj.T)
    dispatch, combine = jnp.swapaxes(dispatch, 1, 2), jnp.swapaxes(combine, 1, 2)
    dispatch_b, combine_b = dispatch.astype(BF), combine.astype(BF)
    sent = shifted(outgoing, out_shift)
    sent, by_image, first, dispatch_b, combine_b, leading = tied(
        sent, by_image, lax.axis_index("y") * 16, dispatch_b, combine_b, core == 0
    )
    got = spread(sent.reshape(2, 8, width)).reshape(256, width)
    parts, rows, hidden, pre_grad = experts(place, got, jnp.swapaxes(in_weight, 1, 2), out_weight)
    scattered = lax.all_to_all(parts.reshape(16, 16, width), PLANE, 0, 0, tiled=True)
    summed = added(scattered.reshape(256, width), 1, 16)
    near = shifted(summed, lambda y, x, c: -out_shift(y, x, c))
    far = shifted(summed, lambda y, x, c: 16 - out_shift(y, x, c))
    home = (near.astype(F32) + far.astype(F32)).astype(BF)
    mine = home.reshape(2, 8, width)
    back = spread(jnp.where(leading, mine, mine[::-1])).reshape(256, width)
    results = picked(by_image, back).reshape(2, 2, 64, width)
    expert_out, slot_grad = results[0], results[1]
    combine_grad = jnp.einsum("itd,ied->ite", out_grad, expert_out, preferred_element_type=F32)
    dispatch_grad = jnp.einsum("itd,ied->ite", tokens, slot_grad, preferred_element_type=F32)
    from_dispatch = dispatch * (dispatch_grad - jnp.sum(dispatch * dispatch_grad, axis=1, keepdims=True))
    from_combine = combine * (combine_grad - jnp.sum(combine * combine_grad, axis=2, keepdims=True))
    logit_grad = (from_dispatch + from_combine).astype(BF)
    own = lax.dynamic_slice(logit_grad, (0, 0, first), (2, 256, 16), allow_negative_indices=False)
    mine = jnp.einsum("ite,itd->ed", own, tokens, preferred_element_type=F32).astype(BF)
    mixed = jnp.einsum("ite,ied->itd", combine_b, expert_out, preferred_element_type=F32).astype(BF)
    mine = added(gathered(mine, ("zr", "c"), 8).reshape(128, width), 1, 16)
    mine, mixed = tied(mine, mixed)
    mine = shifted(mine, lambda y, x, c: 4 * (0, 1, 2, -1)[x] * (1 - 2 * c))
    mine, logit_grad, slot_grad, rows, hidden, pre_grad = tied(mine, logit_grad, slot_grad, rows, hidden, pre_grad)
    shares = gathered(mine, PLANE, 16).reshape(256, width)
    slots, cotangents = rows[:, :64], rows[:, 64:]
    out_weight_grad = jnp.einsum("erf,erd->efd", hidden, cotangents, preferred_element_type=F32).astype(BF)
    in_weight_grad = jnp.einsum("erd,erf->edf", slots, pre_grad, preferred_element_type=F32).astype(BF)
    weights = jnp.concatenate([dispatch_b, logit_grad], axis=2)
    vectors = jnp.concatenate([slot_grad, jnp.broadcast_to(slot_proj.T, (2, 64, width))], axis=1)
    token_grad = jnp.einsum("itk,ikd->itd", weights, vectors, preferred_element_type=F32).astype(BF)
    proj_grad = added(shares, 4, 16).T
    return (mixed, token_grad, proj_grad, in_weight_grad, out_weight_grad)


def solution(mesh):
    fine = Mesh(mesh.devices.reshape(4, 2, 4, 4, 4, 2), ALL)
    images, first, second = P(EXP, None, None), P(EXP, None, REP), P(EXP, REP, None)
    return jax.shard_map(
        on_device,
        mesh=fine,
        in_specs=(images, P(), first, second, images),
        out_specs=(images, images, P(), first, second),
        check_vma=False,
    )
```

```python
import jax
import jax.numpy as jnp
import numpy as np
from jax import lax
from jax.experimental import pallas as pl
from jax.experimental.pallas import tpu as pltpu
from jax.sharding import Mesh, PartitionSpec as P

ALL = ("y", "zh", "x", "zq", "zr", "c")
PLANE = ("y", "x")
EXP = ("zq", "zr", "c")
REP = ("y", "zh", "x")
BF = jnp.bfloat16
F32 = jnp.float32


def signed(r):
    return r if r <= 8 else r - 16


def shifted(value, shift):
    pairs = []
    for y in range(4):
        for x in range(4):
            for z in range(32):
                for c in range(2):
                    to = (z + shift(y, x, z, c)) % 32
                    source = (((y * 2 + z // 16) * 4 + x) * 16 + z % 16) * 2 + c
                    target = (((y * 2 + to // 16) * 4 + x) * 16 + to % 16) * 2 + c
                    pairs.append((source, target))
    return lax.ppermute(value, ALL, pairs)


def out_shift(y, x, z, c):
    return signed(4 * y + x) * (1 - 2 * c)


def group_shift(y, x, z, c):
    return (0, 4 - 8 * c, 6 if z % 4 >= 2 else -6, 8 * c - 4)[x]


def spread(rows):
    out = jnp.broadcast_to(rows[None], (16,) + rows.shape).reshape((32,) + rows.shape[1:])
    return lax.all_to_all(out, PLANE + ("c",), 0, 0, tiled=True)


def chooser(index, size):
    return (index[:, None] == jnp.arange(size)[None, :]).astype(BF)


def picked(choose, rows):
    return jnp.dot(choose, rows, preferred_element_type=F32).astype(BF)


def added(rows, groups, inner):
    to, source = np.arange(groups * inner), np.arange(rows.shape[0])
    span = rows.shape[0] // groups
    same = (source[None, :] // span == to[:, None] // inner) & (source[None, :] % inner == to[:, None] % inner)
    return jnp.dot(jnp.asarray(same.astype(BF)), rows, preferred_element_type=F32).astype(BF)


def tied(*values):
    return lax.optimization_barrier(values)


def gathered(value, axes, size):
    out = jnp.broadcast_to(value[None], (size,) + value.shape)
    return lax.all_to_all(out, axes, 0, 0, tiled=True)


def front_body(place_ref, tokens_ref, cotangent_ref, proj_ref, sent_ref, dispatch_ref, combine_ref, rows_ref):
    for image in range(2):
        tokens = tokens_ref[image]
        logits = lax.dot_general(proj_ref[...], tokens, (((1,), (1,)), ((), ())), preferred_element_type=F32)
        raised = jnp.exp(logits - jnp.max(logits, axis=1, keepdims=True))
        dispatch = raised / jnp.sum(raised, axis=1, keepdims=True)
        raised = jnp.exp(logits - jnp.max(logits, axis=0, keepdims=True))
        combine = raised / jnp.sum(raised, axis=0, keepdims=True)
        dispatch_ref[image] = dispatch
        combine_ref[image] = combine
        rows_ref[64 * image : 64 * image + 64, :] = jnp.dot(
            dispatch.astype(BF), tokens, preferred_element_type=F32
        ).astype(BF)
        rows_ref[64 * image + 128 : 64 * image + 192, :] = jnp.dot(
            combine.astype(BF), cotangent_ref[image], preferred_element_type=F32
        ).astype(BF)
    z_lo, column, core = place_ref[0], place_ref[1], place_ref[2]
    row = lax.broadcasted_iota(jnp.int32, (16, 256), 0)
    target = (z_lo + (1 - 2 * core) * column) & 15
    wanted = ((row >> 2) & 1) * 128 + (row & 1) * 64 + 4 * target + (row >> 3) * 2 + ((row >> 1) & 1)
    choose = (wanted == lax.broadcasted_iota(jnp.int32, (16, 256), 1)).astype(F32).astype(BF)
    sent_ref[...] = jnp.dot(choose, rows_ref[...], preferred_element_type=F32).astype(BF)


def front(place, tokens, cotangent, proj):
    width = tokens.shape[2]
    vmem = pl.BlockSpec(memory_space=pltpu.VMEM)
    return pl.pallas_call(
        front_body,
        in_specs=[pl.BlockSpec(memory_space=pltpu.SMEM), vmem, vmem, vmem],
        out_specs=[vmem, vmem, vmem],
        out_shape=[
            jax.ShapeDtypeStruct((16, width), BF),
            jax.ShapeDtypeStruct((2, 64, 256), F32),
            jax.ShapeDtypeStruct((2, 64, 256), F32),
        ],
        scratch_shapes=[pltpu.VMEM((256, width), BF)],
        compiler_params=pltpu.CompilerParams(vmem_limit_bytes=56 * 2**20),
    )(place, tokens, cotangent, proj)


def experts_body(place_ref, got_ref, first_ref, second_ref, out_ref, rows_ref, hidden_ref, grad_ref, parts_ref):
    which = pl.program_id(0)
    row = lax.broadcasted_iota(jnp.int32, (128, 256), 0)
    wanted = ((row >> 1) & 31) * 8 + (row >> 6) * 4 + which * 2 + (row & 1)
    choose = (wanted == lax.broadcasted_iota(jnp.int32, (128, 256), 1)).astype(F32).astype(BF)
    rows = jnp.dot(choose, got_ref[...], preferred_element_type=F32).astype(BF)
    rows_ref[0] = rows
    slots, cotangents = rows[:64], rows[64:]
    first, second = first_ref[0], second_ref[0]
    turned = (((1,), (1,)), ((), ()))
    v = lax.dot_general(slots, first, turned, preferred_element_type=F32)
    hidden_grad = lax.dot_general(cotangents, second, turned, preferred_element_type=F32)
    root = 0.7978845608028654
    square = v * v
    t = jnp.tanh(root * v * (1.0 + 0.044715 * square))
    hidden = (0.5 * v * (1.0 + t)).astype(BF)
    slope = 0.5 * (1.0 + t) + 0.5 * v * (1.0 - t * t) * (root * (1.0 + 3.0 * 0.044715 * square))
    pre_grad = (hidden_grad * slope).astype(BF)
    hidden_ref[0] = hidden
    grad_ref[0] = pre_grad
    start = pl.multiple_of(which * 128, 128)
    parts_ref[pl.ds(start, 64), :] = jnp.dot(hidden, second, preferred_element_type=F32).astype(BF)
    parts_ref[pl.ds(start + 64, 64), :] = jnp.dot(pre_grad, first, preferred_element_type=F32).astype(BF)

    @pl.when(which == 1)
    def _():
        core = place_ref[2]
        row = lax.broadcasted_iota(jnp.int32, (256, 256), 0)
        other = (row >> 3) & 1
        to = row >> 4
        source = jnp.where(other == 1, (16 - to) & 15, to)
        image_core = jnp.where(other == 1, 1 - core, core)
        wanted = ((row >> 1) & 1) * 128 + ((row >> 2) & 1) * 64 + source * 4 + image_core * 2 + (row & 1)
        choose = (wanted == lax.broadcasted_iota(jnp.int32, (256, 256), 1)).astype(F32).astype(BF)
        out_ref[...] = jnp.dot(choose, parts_ref[...], preferred_element_type=F32).astype(BF)


def experts(place, got, first, second):
    width = got.shape[1]
    units = first.shape[1]
    whole = pl.BlockSpec((256, width), lambda i: (0, 0))
    weight = pl.BlockSpec((1, units, width), lambda i: (i, 0, 0))
    act = pl.BlockSpec((1, 64, units), lambda i: (i, 0, 0))
    return pl.pallas_call(
        experts_body,
        grid=(2,),
        in_specs=[pl.BlockSpec(memory_space=pltpu.SMEM), whole, weight, weight],
        out_specs=[whole, pl.BlockSpec((1, 128, width), lambda i: (i, 0, 0)), act, act],
        out_shape=[
            jax.ShapeDtypeStruct((256, width), BF),
            jax.ShapeDtypeStruct((2, 128, width), BF),
            jax.ShapeDtypeStruct((2, 64, units), BF),
            jax.ShapeDtypeStruct((2, 64, units), BF),
        ],
        scratch_shapes=[pltpu.VMEM((256, width), BF)],
        compiler_params=pltpu.CompilerParams(vmem_limit_bytes=24 * 2**20),
    )(place, got, first, second)


def on_device(tokens, slot_proj, in_weight, out_weight, out_grad):
    width = tokens.shape[2]
    column = lax.axis_index("y") * 4 + lax.axis_index("x")
    core = lax.axis_index("c")
    z_lo = lax.axis_index("zq") * 4 + lax.axis_index("zr")
    row = jnp.arange(256)
    expert = row % 64
    core_of = (expert // 2) % 2
    source = ((1 - 2 * core_of) * (expert // 4 - z_lo)) % 16
    by_image = chooser(
        source * 16 + core_of * 8 + row // 128 * 4 + expert % 2 * 2 + (row // 64) % 2, 256
    )

    place = jnp.stack([z_lo, column, core]).astype(jnp.int32)
    outgoing, dispatch, combine = front(place, tokens, out_grad, slot_proj.T)
    dispatch, combine = jnp.swapaxes(dispatch, 1, 2), jnp.swapaxes(combine, 1, 2)
    dispatch_b, combine_b = dispatch.astype(BF), combine.astype(BF)
    sent = shifted(outgoing, out_shift)
    sent, by_image, first, dispatch_b, combine_b, leading = tied(
        sent, by_image, lax.axis_index("y") * 16, dispatch_b, combine_b, core == 0
    )
    got = spread(sent.reshape(2, 8, width)).reshape(256, width)
    parts, rows, hidden, pre_grad = experts(place, got, jnp.swapaxes(in_weight, 1, 2), out_weight)
    scattered = lax.all_to_all(parts.reshape(16, 16, width), PLANE, 0, 0, tiled=True)
    summed = added(scattered.reshape(256, width), 1, 16)
    near = shifted(summed, lambda y, x, z, c: -out_shift(y, x, z, c))
    far = shifted(summed, lambda y, x, z, c: 16 - out_shift(y, x, z, c))
    home = (near.astype(F32) + far.astype(F32)).astype(BF)
    mine = home.reshape(2, 8, width)
    back = spread(jnp.where(leading, mine, mine[::-1])).reshape(256, width)
    results = picked(by_image, back).reshape(2, 2, 64, width)
    expert_out, slot_grad = results[0], results[1]
    combine_grad = jnp.einsum("itd,ied->ite", out_grad, expert_out, preferred_element_type=F32)
    dispatch_grad = jnp.einsum("itd,ied->ite", tokens, slot_grad, preferred_element_type=F32)
    from_dispatch = dispatch * (dispatch_grad - jnp.sum(dispatch * dispatch_grad, axis=1, keepdims=True))
    from_combine = combine * (combine_grad - jnp.sum(combine * combine_grad, axis=2, keepdims=True))
    logit_grad = (from_dispatch + from_combine).astype(BF)
    own = lax.dynamic_slice(logit_grad, (0, 0, first), (2, 256, 16), allow_negative_indices=False)
    mine = jnp.einsum("ite,itd->ed", own, tokens, preferred_element_type=F32).astype(BF)
    mixed = jnp.einsum("ite,ied->itd", combine_b, expert_out, preferred_element_type=F32).astype(BF)
    other = lax.ppermute(mine, "c", [(0, 1), (1, 0)])
    mine = (mine.astype(F32) + other.astype(F32)).astype(BF)
    mine = added(gathered(mine, "zr", 4).reshape(64, width), 1, 16)
    mine, mixed = tied(mine, mixed)
    mine = shifted(mine, group_shift)
    mine, logit_grad, slot_grad, rows, hidden, pre_grad = tied(mine, logit_grad, slot_grad, rows, hidden, pre_grad)
    shares = gathered(mine, PLANE, 16).reshape(256, width)
    slots, cotangents = rows[:, :64], rows[:, 64:]
    out_weight_grad = jnp.einsum("erf,erd->efd", hidden, cotangents, preferred_element_type=F32).astype(BF)
    in_weight_grad = jnp.einsum("erd,erf->edf", slots, pre_grad, preferred_element_type=F32).astype(BF)
    weights = jnp.concatenate([dispatch_b, logit_grad], axis=2)
    vectors = jnp.concatenate([slot_grad, jnp.broadcast_to(slot_proj.T, (2, 64, width))], axis=1)
    token_grad = jnp.einsum("itk,ikd->itd", weights, vectors, preferred_element_type=F32).astype(BF)
    proj_grad = added(shares, 4, 16).T
    return (mixed, token_grad, proj_grad, in_weight_grad, out_weight_grad)


def solution(mesh):
    fine = Mesh(mesh.devices.reshape(4, 2, 4, 4, 4, 2), ALL)
    images, first, second = P(EXP, None, None), P(EXP, None, REP), P(EXP, REP, None)
    return jax.shard_map(
        on_device,
        mesh=fine,
        in_specs=(images, P(), first, second, images),
        out_specs=(images, images, P(), first, second),
        check_vma=False,
    )
```

```python
import jax
import jax.numpy as jnp
import numpy as np
from jax import lax
from jax.experimental import pallas as pl
from jax.experimental.pallas import tpu as pltpu
from jax.sharding import Mesh, PartitionSpec as P

ALL = ("y", "zh", "x", "zq", "zr", "c")
PLANE = ("y", "x")
EXP = ("zq", "zr", "c")
REP = ("y", "zh", "x")
BF = jnp.bfloat16
F32 = jnp.float32


def signed(r):
    return r if r <= 8 else r - 16


def shifted(value, shift):
    pairs = []
    for y in range(4):
        for x in range(4):
            for z in range(32):
                for c in range(2):
                    to = (z + shift(y, x, z, c)) % 32
                    source = (((y * 2 + z // 16) * 4 + x) * 16 + z % 16) * 2 + c
                    target = (((y * 2 + to // 16) * 4 + x) * 16 + to % 16) * 2 + c
                    pairs.append((source, target))
    return lax.ppermute(value, ALL, pairs)


def out_shift(y, x, z, c):
    return signed(4 * y + x) * (1 - 2 * c)


def group_shift(y, x, z, c):
    return (0, 4 - 8 * c, 6 if z % 4 >= 2 else -6, 8 * c - 4)[x]


def spread(rows):
    out = jnp.broadcast_to(rows[None], (16,) + rows.shape).reshape((32,) + rows.shape[1:])
    return lax.all_to_all(out, PLANE + ("c",), 0, 0, tiled=True)


def chooser(index, size):
    return (index[:, None] == jnp.arange(size)[None, :]).astype(BF)


def picked(choose, rows):
    return jnp.dot(choose, rows, preferred_element_type=F32).astype(BF)


def added(rows, groups, inner):
    to, source = np.arange(groups * inner), np.arange(rows.shape[0])
    span = rows.shape[0] // groups
    same = (source[None, :] // span == to[:, None] // inner) & (source[None, :] % inner == to[:, None] % inner)
    return jnp.dot(jnp.asarray(same.astype(BF)), rows, preferred_element_type=F32).astype(BF)


def tied(*values):
    return lax.optimization_barrier(values)


def gathered(value, axes, size):
    out = jnp.broadcast_to(value[None], (size,) + value.shape)
    return lax.all_to_all(out, axes, 0, 0, tiled=True)


def front_body(place_ref, tokens_ref, cotangent_ref, proj_ref, sent_ref, dispatch_ref, combine_ref, rows_ref):
    for image in range(2):
        tokens = tokens_ref[image]
        logits = lax.dot_general(proj_ref[...], tokens, (((1,), (1,)), ((), ())), preferred_element_type=F32)
        raised = jnp.exp(logits - jnp.max(logits, axis=1, keepdims=True))
        dispatch = raised / jnp.sum(raised, axis=1, keepdims=True)
        raised = jnp.exp(logits - jnp.max(logits, axis=0, keepdims=True))
        combine = raised / jnp.sum(raised, axis=0, keepdims=True)
        dispatch_ref[image] = dispatch
        combine_ref[image] = combine
        rows_ref[64 * image : 64 * image + 64, :] = jnp.dot(
            dispatch.astype(BF), tokens, preferred_element_type=F32
        ).astype(BF)
        rows_ref[64 * image + 128 : 64 * image + 192, :] = jnp.dot(
            combine.astype(BF), cotangent_ref[image], preferred_element_type=F32
        ).astype(BF)
    z_lo, column, core = place_ref[0], place_ref[1], place_ref[2]
    row = lax.broadcasted_iota(jnp.int32, (16, 256), 0)
    near = (z_lo + (1 - 2 * core) * column) & 15
    cross = (z_lo - (1 - 2 * core) * column) & 15
    block = jnp.where(row < 8, 4 * near + 2 * core, 4 * cross + 2 * (1 - core))
    wanted = ((row >> 2) & 1) * 128 + (row & 1) * 64 + block + ((row >> 1) & 1)
    choose = (wanted == lax.broadcasted_iota(jnp.int32, (16, 256), 1)).astype(F32).astype(BF)
    sent_ref[...] = jnp.dot(choose, rows_ref[...], preferred_element_type=F32).astype(BF)


def front(place, tokens, cotangent, proj):
    width = tokens.shape[2]
    vmem = pl.BlockSpec(memory_space=pltpu.VMEM)
    return pl.pallas_call(
        front_body,
        in_specs=[pl.BlockSpec(memory_space=pltpu.SMEM), vmem, vmem, vmem],
        out_specs=[vmem, vmem, vmem],
        out_shape=[
            jax.ShapeDtypeStruct((16, width), BF),
            jax.ShapeDtypeStruct((2, 64, 256), F32),
            jax.ShapeDtypeStruct((2, 64, 256), F32),
        ],
        scratch_shapes=[pltpu.VMEM((256, width), BF)],
        compiler_params=pltpu.CompilerParams(vmem_limit_bytes=56 * 2**20),
    )(place, tokens, cotangent, proj)


def experts_body(got_ref, first_ref, second_ref, out_ref, rows_ref, hidden_ref, grad_ref, parts_ref):
    which = pl.program_id(0)
    row = lax.broadcasted_iota(jnp.int32, (128, 256), 0)
    wanted = ((row >> 1) & 31) * 8 + (row >> 6) * 4 + which * 2 + (row & 1)
    choose = (wanted == lax.broadcasted_iota(jnp.int32, (128, 256), 1)).astype(F32).astype(BF)
    rows = jnp.dot(choose, got_ref[...], preferred_element_type=F32).astype(BF)
    rows_ref[0] = rows
    slots, cotangents = rows[:64], rows[64:]
    first, second = first_ref[0], second_ref[0]
    turned = (((1,), (1,)), ((), ()))
    v = lax.dot_general(slots, first, turned, preferred_element_type=F32)
    hidden_grad = lax.dot_general(cotangents, second, turned, preferred_element_type=F32)
    root = 0.7978845608028654
    square = v * v
    t = jnp.tanh(root * v * (1.0 + 0.044715 * square))
    hidden = (0.5 * v * (1.0 + t)).astype(BF)
    slope = 0.5 * (1.0 + t) + 0.5 * v * (1.0 - t * t) * (root * (1.0 + 3.0 * 0.044715 * square))
    pre_grad = (hidden_grad * slope).astype(BF)
    hidden_ref[0] = hidden
    grad_ref[0] = pre_grad
    start = pl.multiple_of(which * 128, 128)
    parts_ref[pl.ds(start, 64), :] = jnp.dot(hidden, second, preferred_element_type=F32).astype(BF)
    parts_ref[pl.ds(start + 64, 64), :] = jnp.dot(pre_grad, first, preferred_element_type=F32).astype(BF)

    @pl.when(which == 1)
    def _():
        row = lax.broadcasted_iota(jnp.int32, (256, 256), 0)
        wanted = ((row >> 1) & 1) * 128 + ((row >> 2) & 1) * 64 + (row >> 3) * 2 + (row & 1)
        choose = (wanted == lax.broadcasted_iota(jnp.int32, (256, 256), 1)).astype(F32).astype(BF)
        out_ref[...] = jnp.dot(choose, parts_ref[...], preferred_element_type=F32).astype(BF)


def experts(got, first, second):
    width = got.shape[1]
    units = first.shape[1]
    whole = pl.BlockSpec((256, width), lambda i: (0, 0))
    weight = pl.BlockSpec((1, units, width), lambda i: (i, 0, 0))
    act = pl.BlockSpec((1, 64, units), lambda i: (i, 0, 0))
    return pl.pallas_call(
        experts_body,
        grid=(2,),
        in_specs=[whole, weight, weight],
        out_specs=[whole, pl.BlockSpec((1, 128, width), lambda i: (i, 0, 0)), act, act],
        out_shape=[
            jax.ShapeDtypeStruct((256, width), BF),
            jax.ShapeDtypeStruct((2, 128, width), BF),
            jax.ShapeDtypeStruct((2, 64, units), BF),
            jax.ShapeDtypeStruct((2, 64, units), BF),
        ],
        scratch_shapes=[pltpu.VMEM((256, width), BF)],
        compiler_params=pltpu.CompilerParams(vmem_limit_bytes=24 * 2**20),
    )(got, first, second)


def on_device(tokens, slot_proj, in_weight, out_weight, out_grad):
    width = tokens.shape[2]
    column = lax.axis_index("y") * 4 + lax.axis_index("x")
    core = lax.axis_index("c")
    z_lo = lax.axis_index("zq") * 4 + lax.axis_index("zr")
    row = jnp.arange(256)
    expert = row % 64
    core_of = (expert // 2) % 2
    source = ((1 - 2 * core_of) * (expert // 4 - z_lo)) % 16
    by_image = chooser(
        source * 16 + core_of * 8 + row // 128 * 4 + expert % 2 * 2 + (row // 64) % 2, 256
    )

    place = jnp.stack([z_lo, column, core]).astype(jnp.int32)
    outgoing, dispatch, combine = front(place, tokens, out_grad, slot_proj.T)
    dispatch, combine = jnp.swapaxes(dispatch, 1, 2), jnp.swapaxes(combine, 1, 2)
    dispatch_b, combine_b = dispatch.astype(BF), combine.astype(BF)
    crossed = lax.ppermute(outgoing, "c", [(0, 1), (1, 0)])
    sent = shifted(jnp.concatenate([outgoing[:8], crossed[8:]]), out_shift)
    sent, by_image, first, dispatch_b, combine_b, leading = tied(
        sent, by_image, lax.axis_index("y") * 16, dispatch_b, combine_b, core == 0
    )
    got = gathered(sent, PLANE, 16).reshape(256, width)
    parts, rows, hidden, pre_grad = experts(got, jnp.swapaxes(in_weight, 1, 2), out_weight)
    scattered = lax.all_to_all(parts.reshape(16, 16, width), PLANE, 0, 0, tiled=True)
    summed = added(scattered.reshape(256, width), 1, 16)
    near = shifted(summed, lambda y, x, z, c: -out_shift(y, x, z, c))
    far = shifted(summed, lambda y, x, z, c: 16 - out_shift(y, x, z, c))
    home = (near.astype(F32) + far.astype(F32)).astype(BF)
    mine = home.reshape(2, 8, width)
    back = spread(jnp.where(leading, mine, mine[::-1])).reshape(256, width)
    results = picked(by_image, back).reshape(2, 2, 64, width)
    expert_out, slot_grad = results[0], results[1]
    combine_grad = jnp.einsum("itd,ied->ite", out_grad, expert_out, preferred_element_type=F32)
    dispatch_grad = jnp.einsum("itd,ied->ite", tokens, slot_grad, preferred_element_type=F32)
    from_dispatch = dispatch * (dispatch_grad - jnp.sum(dispatch * dispatch_grad, axis=1, keepdims=True))
    from_combine = combine * (combine_grad - jnp.sum(combine * combine_grad, axis=2, keepdims=True))
    logit_grad = (from_dispatch + from_combine).astype(BF)
    own = lax.dynamic_slice(logit_grad, (0, 0, first), (2, 256, 16), allow_negative_indices=False)
    mine = jnp.einsum("ite,itd->ed", own, tokens, preferred_element_type=F32).astype(BF)
    mixed = jnp.einsum("ite,ied->itd", combine_b, expert_out, preferred_element_type=F32).astype(BF)
    other = lax.ppermute(mine, "c", [(0, 1), (1, 0)])
    mine = (mine.astype(F32) + other.astype(F32)).astype(BF)
    mine = added(gathered(mine, "zr", 4).reshape(64, width), 1, 16)
    mine, mixed = tied(mine, mixed)
    mine = shifted(mine, group_shift)
    mine, logit_grad, slot_grad, rows, hidden, pre_grad = tied(mine, logit_grad, slot_grad, rows, hidden, pre_grad)
    shares = gathered(mine, PLANE, 16).reshape(256, width)
    slots, cotangents = rows[:, :64], rows[:, 64:]
    out_weight_grad = jnp.einsum("erf,erd->efd", hidden, cotangents, preferred_element_type=F32).astype(BF)
    in_weight_grad = jnp.einsum("erd,erf->edf", slots, pre_grad, preferred_element_type=F32).astype(BF)
    weights = jnp.concatenate([dispatch_b, logit_grad], axis=2)
    vectors = jnp.concatenate([slot_grad, jnp.broadcast_to(slot_proj.T, (2, 64, width))], axis=1)
    token_grad = jnp.einsum("itk,ikd->itd", weights, vectors, preferred_element_type=F32).astype(BF)
    proj_grad = added(shares, 4, 16).T
    return (mixed, token_grad, proj_grad, in_weight_grad, out_weight_grad)


def solution(mesh):
    fine = Mesh(mesh.devices.reshape(4, 2, 4, 4, 4, 2), ALL)
    images, first, second = P(EXP, None, None), P(EXP, None, REP), P(EXP, REP, None)
    return jax.shard_map(
        on_device,
        mesh=fine,
        in_specs=(images, P(), first, second, images),
        out_specs=(images, images, P(), first, second),
        check_vma=False,
    )
```

```python
import jax
import jax.numpy as jnp
import numpy as np
from jax import lax
from jax.experimental import pallas as pl
from jax.experimental.pallas import tpu as pltpu
from jax.sharding import Mesh, PartitionSpec as P

ALL = ("y", "zh", "x", "zq", "zr", "c")
PLANE = ("y", "x")
EXP = ("zq", "zr", "c")
REP = ("y", "zh", "x")
BF = jnp.bfloat16
F32 = jnp.float32


def signed(r):
    return r if r <= 8 else r - 16


def shifted(value, shift):
    pairs = []
    for y in range(4):
        for x in range(4):
            for z in range(32):
                for c in range(2):
                    to = (z + shift(y, x, z, c)) % 32
                    source = (((y * 2 + z // 16) * 4 + x) * 16 + z % 16) * 2 + c
                    target = (((y * 2 + to // 16) * 4 + x) * 16 + to % 16) * 2 + c
                    pairs.append((source, target))
    return lax.ppermute(value, ALL, pairs)


def out_shift(y, x, z, c):
    return signed(4 * y + x) * (1 - 2 * c)


def group_shift(y, x, z, c):
    return (0, 4 - 8 * c, 6 if z % 4 >= 2 else -6, 8 * c - 4)[x]


def spread(rows):
    out = jnp.broadcast_to(rows[None], (16,) + rows.shape).reshape((32,) + rows.shape[1:])
    return lax.all_to_all(out, PLANE + ("c",), 0, 0, tiled=True)


def chooser(index, size):
    return (index[:, None] == jnp.arange(size)[None, :]).astype(BF)


def picked(choose, rows):
    return jnp.dot(choose, rows, preferred_element_type=F32).astype(BF)


def added(rows, groups, inner):
    to, source = np.arange(groups * inner), np.arange(rows.shape[0])
    span = rows.shape[0] // groups
    same = (source[None, :] // span == to[:, None] // inner) & (source[None, :] % inner == to[:, None] % inner)
    return jnp.dot(jnp.asarray(same.astype(BF)), rows, preferred_element_type=F32).astype(BF)


def tied(*values):
    return lax.optimization_barrier(values)


def gathered(value, axes, size):
    out = jnp.broadcast_to(value[None], (size,) + value.shape)
    return lax.all_to_all(out, axes, 0, 0, tiled=True)


def front_body(z_ref, column_ref, core_ref, tokens_ref, cotangent_ref, proj_ref, sent_ref, dispatch_ref, combine_ref, rows_ref):
    for image in range(2):
        tokens = tokens_ref[image]
        logits = lax.dot_general(proj_ref[...], tokens, (((1,), (1,)), ((), ())), preferred_element_type=F32)
        raised = jnp.exp(logits - jnp.max(logits, axis=1, keepdims=True))
        dispatch = raised / jnp.sum(raised, axis=1, keepdims=True)
        raised = jnp.exp(logits - jnp.max(logits, axis=0, keepdims=True))
        combine = raised / jnp.sum(raised, axis=0, keepdims=True)
        dispatch_ref[image] = dispatch
        combine_ref[image] = combine
        rows_ref[64 * image : 64 * image + 64, :] = jnp.dot(
            dispatch.astype(BF), tokens, preferred_element_type=F32
        ).astype(BF)
        rows_ref[64 * image + 128 : 64 * image + 192, :] = jnp.dot(
            combine.astype(BF), cotangent_ref[image], preferred_element_type=F32
        ).astype(BF)
    z_lo, column, core = z_ref[0], column_ref[0], core_ref[0]
    row = lax.broadcasted_iota(jnp.int32, (16, 256), 0)
    near = (z_lo + (1 - 2 * core) * column) & 15
    cross = (z_lo - (1 - 2 * core) * column) & 15
    block = jnp.where(row < 8, 4 * near + 2 * core, 4 * cross + 2 * (1 - core))
    wanted = ((row >> 2) & 1) * 128 + (row & 1) * 64 + block + ((row >> 1) & 1)
    choose = (wanted == lax.broadcasted_iota(jnp.int32, (16, 256), 1)).astype(F32).astype(BF)
    sent_ref[...] = jnp.dot(choose, rows_ref[...], preferred_element_type=F32).astype(BF)


def front(places, tokens, cotangent, proj):
    width = tokens.shape[2]
    vmem = pl.BlockSpec(memory_space=pltpu.VMEM)
    return pl.pallas_call(
        front_body,
        in_specs=[pl.BlockSpec(memory_space=pltpu.SMEM)] * 3 + [vmem] * 3,
        out_specs=[vmem, vmem, vmem],
        out_shape=[
            jax.ShapeDtypeStruct((16, width), BF),
            jax.ShapeDtypeStruct((2, 64, 256), F32),
            jax.ShapeDtypeStruct((2, 64, 256), F32),
        ],
        scratch_shapes=[pltpu.VMEM((256, width), BF)],
        compiler_params=pltpu.CompilerParams(vmem_limit_bytes=56 * 2**20),
    )(*places, tokens, cotangent, proj)


def experts_body(got_ref, first_ref, second_ref, out_ref, rows_ref, hidden_ref, grad_ref, parts_ref):
    which = pl.program_id(0)
    row = lax.broadcasted_iota(jnp.int32, (128, 256), 0)
    wanted = ((row >> 1) & 31) * 8 + (row >> 6) * 4 + which * 2 + (row & 1)
    choose = (wanted == lax.broadcasted_iota(jnp.int32, (128, 256), 1)).astype(F32).astype(BF)
    rows = jnp.dot(choose, got_ref[...], preferred_element_type=F32).astype(BF)
    rows_ref[0] = rows
    slots, cotangents = rows[:64], rows[64:]
    first, second = first_ref[0], second_ref[0]
    turned = (((1,), (1,)), ((), ()))
    v = lax.dot_general(slots, first, turned, preferred_element_type=F32)
    hidden_grad = lax.dot_general(cotangents, second, turned, preferred_element_type=F32)
    root = 0.7978845608028654
    square = v * v
    t = jnp.tanh(root * v * (1.0 + 0.044715 * square))
    hidden = (0.5 * v * (1.0 + t)).astype(BF)
    slope = 0.5 * (1.0 + t) + 0.5 * v * (1.0 - t * t) * (root * (1.0 + 3.0 * 0.044715 * square))
    pre_grad = (hidden_grad * slope).astype(BF)
    hidden_ref[0] = hidden
    grad_ref[0] = pre_grad
    start = pl.multiple_of(which * 128, 128)
    parts_ref[pl.ds(start, 64), :] = jnp.dot(hidden, second, preferred_element_type=F32).astype(BF)
    parts_ref[pl.ds(start + 64, 64), :] = jnp.dot(pre_grad, first, preferred_element_type=F32).astype(BF)

    @pl.when(which == 1)
    def _():
        row = lax.broadcasted_iota(jnp.int32, (256, 256), 0)
        wanted = ((row >> 1) & 1) * 128 + ((row >> 2) & 1) * 64 + (row >> 3) * 2 + (row & 1)
        choose = (wanted == lax.broadcasted_iota(jnp.int32, (256, 256), 1)).astype(F32).astype(BF)
        out_ref[...] = jnp.dot(choose, parts_ref[...], preferred_element_type=F32).astype(BF)


def experts(got, first, second):
    width = got.shape[1]
    units = first.shape[1]
    whole = pl.BlockSpec((256, width), lambda i: (0, 0))
    weight = pl.BlockSpec((1, units, width), lambda i: (i, 0, 0))
    act = pl.BlockSpec((1, 64, units), lambda i: (i, 0, 0))
    return pl.pallas_call(
        experts_body,
        grid=(2,),
        in_specs=[whole, weight, weight],
        out_specs=[whole, pl.BlockSpec((1, 128, width), lambda i: (i, 0, 0)), act, act],
        out_shape=[
            jax.ShapeDtypeStruct((256, width), BF),
            jax.ShapeDtypeStruct((2, 128, width), BF),
            jax.ShapeDtypeStruct((2, 64, units), BF),
            jax.ShapeDtypeStruct((2, 64, units), BF),
        ],
        scratch_shapes=[pltpu.VMEM((256, width), BF)],
        compiler_params=pltpu.CompilerParams(vmem_limit_bytes=24 * 2**20),
    )(got, first, second)


def on_device(tokens, slot_proj, in_weight, out_weight, out_grad):
    width = tokens.shape[2]
    column = lax.axis_index("y") * 4 + lax.axis_index("x")
    core = lax.axis_index("c")
    z_lo = lax.axis_index("zq") * 4 + lax.axis_index("zr")
    row = jnp.arange(256)
    expert = row % 64
    core_of = (expert // 2) % 2
    source = ((1 - 2 * core_of) * (expert // 4 - z_lo)) % 16
    by_image = chooser(
        source * 16 + core_of * 8 + row // 128 * 4 + expert % 2 * 2 + (row // 64) % 2, 256
    )

    places = [value.astype(jnp.int32).reshape(1) for value in (z_lo, column, core)]
    outgoing, dispatch, combine = front(places, tokens, out_grad, slot_proj.T)
    dispatch, combine = jnp.swapaxes(dispatch, 1, 2), jnp.swapaxes(combine, 1, 2)
    crossed = lax.ppermute(outgoing, "c", [(0, 1), (1, 0)])
    sent, dispatch, combine = tied(jnp.concatenate([outgoing[:8], crossed[8:]]), dispatch, combine)
    dispatch_b, combine_b = dispatch.astype(BF), combine.astype(BF)
    sent = shifted(sent, out_shift)
    sent, by_image, first, dispatch_b, combine_b, leading = tied(
        sent, by_image, lax.axis_index("y") * 16, dispatch_b, combine_b, core == 0
    )
    got = gathered(sent, PLANE, 16).reshape(256, width)
    parts, rows, hidden, pre_grad = experts(got, jnp.swapaxes(in_weight, 1, 2), out_weight)
    scattered = lax.all_to_all(parts.reshape(16, 16, width), PLANE, 0, 0, tiled=True)
    summed = added(scattered.reshape(256, width), 1, 16)
    near = shifted(summed, lambda y, x, z, c: -out_shift(y, x, z, c))
    far = shifted(summed, lambda y, x, z, c: 16 - out_shift(y, x, z, c))
    home = (near.astype(F32) + far.astype(F32)).astype(BF)
    mine = home.reshape(2, 8, width)
    back = spread(jnp.where(leading, mine, mine[::-1])).reshape(256, width)
    results = picked(by_image, back).reshape(2, 2, 64, width)
    expert_out, slot_grad = results[0], results[1]
    combine_grad = jnp.einsum("itd,ied->ite", out_grad, expert_out, preferred_element_type=F32)
    dispatch_grad = jnp.einsum("itd,ied->ite", tokens, slot_grad, preferred_element_type=F32)
    from_dispatch = dispatch * (dispatch_grad - jnp.sum(dispatch * dispatch_grad, axis=1, keepdims=True))
    from_combine = combine * (combine_grad - jnp.sum(combine * combine_grad, axis=2, keepdims=True))
    logit_grad = (from_dispatch + from_combine).astype(BF)
    own = lax.dynamic_slice(logit_grad, (0, 0, first), (2, 256, 16), allow_negative_indices=False)
    mine = jnp.einsum("ite,itd->ed", own, tokens, preferred_element_type=F32).astype(BF)
    other = lax.ppermute(mine, "c", [(0, 1), (1, 0)])
    mine = (mine.astype(F32) + other.astype(F32)).astype(BF)
    mine = added(gathered(mine, "zr", 4).reshape(64, width), 1, 16)
    mine = shifted(mine, group_shift)
    mine, logit_grad, expert_out, slot_grad, rows, hidden, pre_grad = tied(
        mine, logit_grad, expert_out, slot_grad, rows, hidden, pre_grad
    )
    shares = gathered(mine, PLANE, 16).reshape(256, width)
    slots, cotangents = rows[:, :64], rows[:, 64:]
    out_weight_grad = jnp.einsum("erf,erd->efd", hidden, cotangents, preferred_element_type=F32).astype(BF)
    in_weight_grad = jnp.einsum("erd,erf->edf", slots, pre_grad, preferred_element_type=F32).astype(BF)
    weights = jnp.concatenate([dispatch_b, logit_grad], axis=2)
    vectors = jnp.concatenate([slot_grad, jnp.broadcast_to(slot_proj.T, (2, 64, width))], axis=1)
    token_grad = jnp.einsum("itk,ikd->itd", weights, vectors, preferred_element_type=F32).astype(BF)
    mixed = jnp.einsum("ite,ied->itd", combine_b, expert_out, preferred_element_type=F32).astype(BF)
    proj_grad = added(shares, 4, 16).T
    return (mixed, token_grad, proj_grad, in_weight_grad, out_weight_grad)


def solution(mesh):
    fine = Mesh(mesh.devices.reshape(4, 2, 4, 4, 4, 2), ALL)
    images, first, second = P(EXP, None, None), P(EXP, None, REP), P(EXP, REP, None)
    return jax.shard_map(
        on_device,
        mesh=fine,
        in_specs=(images, P(), first, second, images),
        out_specs=(images, images, P(), first, second),
        check_vma=False,
    )
```

```python
import jax
import jax.numpy as jnp
import numpy as np
from jax import lax
from jax.experimental import pallas as pl
from jax.experimental.pallas import tpu as pltpu
from jax.sharding import Mesh, PartitionSpec as P

ALL = ("y", "zh", "x", "zq", "zr", "c")
PLANE = ("y", "x")
EXP = ("zq", "zr", "c")
REP = ("y", "zh", "x")
BF = jnp.bfloat16
F32 = jnp.float32


def signed(r):
    return r if r <= 8 else r - 16


def shifted(value, shift):
    pairs = []
    for y in range(4):
        for x in range(4):
            for z in range(32):
                for c in range(2):
                    to = (z + shift(y, x, z, c)) % 32
                    source = (((y * 2 + z // 16) * 4 + x) * 16 + z % 16) * 2 + c
                    target = (((y * 2 + to // 16) * 4 + x) * 16 + to % 16) * 2 + c
                    pairs.append((source, target))
    return lax.ppermute(value, ALL, pairs)


def out_shift(y, x, z, c):
    return signed(4 * y + x) * (1 - 2 * c)


def group_shift(y, x, z, c):
    return (0, 4 - 8 * c, 6 if z % 4 >= 2 else -6, 8 * c - 4)[x]


def spread(rows):
    out = jnp.broadcast_to(rows[None], (16,) + rows.shape).reshape((32,) + rows.shape[1:])
    return lax.all_to_all(out, PLANE + ("c",), 0, 0, tiled=True)


def chooser(index, size):
    return (index[:, None] == jnp.arange(size)[None, :]).astype(BF)


def picked(choose, rows):
    return jnp.dot(choose, rows, preferred_element_type=F32).astype(BF)


def added(rows, groups, inner):
    to, source = np.arange(groups * inner), np.arange(rows.shape[0])
    span = rows.shape[0] // groups
    same = (source[None, :] // span == to[:, None] // inner) & (source[None, :] % inner == to[:, None] % inner)
    return jnp.dot(jnp.asarray(same.astype(BF)), rows, preferred_element_type=F32).astype(BF)


def tied(*values):
    return lax.optimization_barrier(values)


def gathered(value, axes, size):
    out = jnp.broadcast_to(value[None], (size,) + value.shape)
    return lax.all_to_all(out, axes, 0, 0, tiled=True)


def front_body(z_ref, column_ref, core_ref, tokens_ref, cotangent_ref, proj_ref, kept_ref, crossing_ref, dispatch_ref, combine_ref, rows_ref):
    for image in range(2):
        tokens = tokens_ref[image]
        logits = lax.dot_general(proj_ref[...], tokens, (((1,), (1,)), ((), ())), preferred_element_type=F32)
        raised = jnp.exp(logits - jnp.max(logits, axis=1, keepdims=True))
        dispatch = raised / jnp.sum(raised, axis=1, keepdims=True)
        raised = jnp.exp(logits - jnp.max(logits, axis=0, keepdims=True))
        combine = raised / jnp.sum(raised, axis=0, keepdims=True)
        dispatch_ref[image] = dispatch
        combine_ref[image] = combine
        rows_ref[64 * image : 64 * image + 64, :] = jnp.dot(
            dispatch.astype(BF), tokens, preferred_element_type=F32
        ).astype(BF)
        rows_ref[64 * image + 128 : 64 * image + 192, :] = jnp.dot(
            combine.astype(BF), cotangent_ref[image], preferred_element_type=F32
        ).astype(BF)
    z_lo, column, core = z_ref[0], column_ref[0], core_ref[0]
    row = lax.broadcasted_iota(jnp.int32, (16, 256), 0)
    near = (z_lo + (1 - 2 * core) * column) & 15
    cross = (z_lo - (1 - 2 * core) * column) & 15
    block = jnp.where(row < 8, 4 * near + 2 * core, 4 * cross + 2 * (1 - core))
    wanted = ((row >> 2) & 1) * 128 + (row & 1) * 64 + block + ((row >> 1) & 1)
    choose = (wanted == lax.broadcasted_iota(jnp.int32, (16, 256), 1)).astype(F32).astype(BF)
    chosen = jnp.dot(choose, rows_ref[...], preferred_element_type=F32)
    own = lax.broadcasted_iota(jnp.int32, chosen.shape, 0) < 8
    kept_ref[...] = jnp.where(own, chosen, 0.0).astype(BF)
    crossing_ref[...] = jnp.where(own, 0.0, chosen).astype(BF)


def front(places, tokens, cotangent, proj):
    width = tokens.shape[2]
    vmem = pl.BlockSpec(memory_space=pltpu.VMEM)
    return pl.pallas_call(
        front_body,
        in_specs=[pl.BlockSpec(memory_space=pltpu.SMEM)] * 3 + [vmem] * 3,
        out_specs=[vmem, vmem, vmem, vmem],
        out_shape=[
            jax.ShapeDtypeStruct((16, width), BF),
            jax.ShapeDtypeStruct((16, width), BF),
            jax.ShapeDtypeStruct((2, 64, 256), F32),
            jax.ShapeDtypeStruct((2, 64, 256), F32),
        ],
        scratch_shapes=[pltpu.VMEM((256, width), BF)],
        compiler_params=pltpu.CompilerParams(vmem_limit_bytes=56 * 2**20),
    )(*places, tokens, cotangent, proj)


def experts_body(got_ref, first_ref, second_ref, out_ref, rows_ref, hidden_ref, grad_ref, parts_ref):
    which = pl.program_id(0)
    row = lax.broadcasted_iota(jnp.int32, (128, 256), 0)
    wanted = ((row >> 1) & 31) * 8 + (row >> 6) * 4 + which * 2 + (row & 1)
    choose = (wanted == lax.broadcasted_iota(jnp.int32, (128, 256), 1)).astype(F32).astype(BF)
    rows = jnp.dot(choose, got_ref[...], preferred_element_type=F32).astype(BF)
    rows_ref[0] = rows
    slots, cotangents = rows[:64], rows[64:]
    first, second = first_ref[0], second_ref[0]
    turned = (((1,), (1,)), ((), ()))
    v = lax.dot_general(slots, first, turned, preferred_element_type=F32)
    hidden_grad = lax.dot_general(cotangents, second, turned, preferred_element_type=F32)
    root = 0.7978845608028654
    square = v * v
    t = jnp.tanh(root * v * (1.0 + 0.044715 * square))
    hidden = (0.5 * v * (1.0 + t)).astype(BF)
    slope = 0.5 * (1.0 + t) + 0.5 * v * (1.0 - t * t) * (root * (1.0 + 3.0 * 0.044715 * square))
    pre_grad = (hidden_grad * slope).astype(BF)
    hidden_ref[0] = hidden
    grad_ref[0] = pre_grad
    start = pl.multiple_of(which * 128, 128)
    parts_ref[pl.ds(start, 64), :] = jnp.dot(hidden, second, preferred_element_type=F32).astype(BF)
    parts_ref[pl.ds(start + 64, 64), :] = jnp.dot(pre_grad, first, preferred_element_type=F32).astype(BF)

    @pl.when(which == 1)
    def _():
        row = lax.broadcasted_iota(jnp.int32, (256, 256), 0)
        wanted = ((row >> 1) & 1) * 128 + ((row >> 2) & 1) * 64 + (row >> 3) * 2 + (row & 1)
        choose = (wanted == lax.broadcasted_iota(jnp.int32, (256, 256), 1)).astype(F32).astype(BF)
        out_ref[...] = jnp.dot(choose, parts_ref[...], preferred_element_type=F32).astype(BF)


def experts(got, first, second):
    width = got.shape[1]
    units = first.shape[1]
    whole = pl.BlockSpec((256, width), lambda i: (0, 0))
    weight = pl.BlockSpec((1, units, width), lambda i: (i, 0, 0))
    act = pl.BlockSpec((1, 64, units), lambda i: (i, 0, 0))
    return pl.pallas_call(
        experts_body,
        grid=(2,),
        in_specs=[whole, weight, weight],
        out_specs=[whole, pl.BlockSpec((1, 128, width), lambda i: (i, 0, 0)), act, act],
        out_shape=[
            jax.ShapeDtypeStruct((256, width), BF),
            jax.ShapeDtypeStruct((2, 128, width), BF),
            jax.ShapeDtypeStruct((2, 64, units), BF),
            jax.ShapeDtypeStruct((2, 64, units), BF),
        ],
        scratch_shapes=[pltpu.VMEM((256, width), BF)],
        compiler_params=pltpu.CompilerParams(vmem_limit_bytes=24 * 2**20),
    )(got, first, second)


def staged_body(tokens_ref, cotangent_ref, tokens_out, cotangent_out):
    tokens_out[...] = tokens_ref[...]
    cotangent_out[...] = cotangent_ref[...]


def staged(tokens, cotangent):
    image = pl.BlockSpec((1,) + tokens.shape[1:], lambda i: (i, 0, 0))
    shape = jax.ShapeDtypeStruct(tokens.shape, tokens.dtype)
    return pl.pallas_call(
        staged_body,
        grid=(2,),
        in_specs=[image, image],
        out_specs=[image, image],
        out_shape=[shape, shape],
        compiler_params=pltpu.CompilerParams(vmem_limit_bytes=24 * 2**20),
    )(tokens, cotangent)


def on_device(tokens, slot_proj, in_weight, out_weight, out_grad):
    width = tokens.shape[2]
    column = lax.axis_index("y") * 4 + lax.axis_index("x")
    core = lax.axis_index("c")
    z_lo = lax.axis_index("zq") * 4 + lax.axis_index("zr")
    row = jnp.arange(256)
    expert = row % 64
    core_of = (expert // 2) % 2
    source = ((1 - 2 * core_of) * (expert // 4 - z_lo)) % 16
    by_image = chooser(
        source * 16 + core_of * 8 + row // 128 * 4 + expert % 2 * 2 + (row // 64) % 2, 256
    )

    places = [value.astype(jnp.int32).reshape(1) for value in (z_lo, column, core)]
    kept, crossing, dispatch, combine = front(places, tokens, out_grad, slot_proj.T)
    dispatch, combine = jnp.swapaxes(dispatch, 1, 2), jnp.swapaxes(combine, 1, 2)
    crossed = lax.ppermute(crossing, "c", [(0, 1), (1, 0)])
    sent, dispatch, combine = tied(kept + crossed, dispatch, combine)
    dispatch_b, combine_b = dispatch.astype(BF), combine.astype(BF)
    sent = shifted(sent, out_shift)
    sent, by_image, first, dispatch_b, combine_b, leading = tied(
        sent, by_image, lax.axis_index("y") * 16, dispatch_b, combine_b, core == 0
    )
    got = gathered(sent, PLANE, 16).reshape(256, width)
    parts, rows, hidden, pre_grad = experts(got, jnp.swapaxes(in_weight, 1, 2), out_weight)
    scattered = lax.all_to_all(parts.reshape(16, 16, width), PLANE, 0, 0, tiled=True)
    summed = added(scattered.reshape(256, width), 1, 16)
    summed, tokens_in, cotangent_in = tied(summed, tokens, out_grad)
    tokens_near, cotangent_near = staged(tokens_in, cotangent_in)
    near = shifted(summed, lambda y, x, z, c: -out_shift(y, x, z, c))
    far = shifted(summed, lambda y, x, z, c: 16 - out_shift(y, x, z, c))
    home = (near.astype(F32) + far.astype(F32)).astype(BF)
    home, tokens_near, cotangent_near = tied(home, tokens_near, cotangent_near)
    mine = home.reshape(2, 8, width)
    back = spread(jnp.where(leading, mine, mine[::-1])).reshape(256, width)
    results = picked(by_image, back).reshape(2, 2, 64, width)
    expert_out, slot_grad = results[0], results[1]
    combine_grad = jnp.einsum("itd,ied->ite", cotangent_near, expert_out, preferred_element_type=F32)
    dispatch_grad = jnp.einsum("itd,ied->ite", tokens_near, slot_grad, preferred_element_type=F32)
    from_dispatch = dispatch * (dispatch_grad - jnp.sum(dispatch * dispatch_grad, axis=1, keepdims=True))
    from_combine = combine * (combine_grad - jnp.sum(combine * combine_grad, axis=2, keepdims=True))
    logit_grad = (from_dispatch + from_combine).astype(BF)
    own = lax.dynamic_slice(logit_grad, (0, 0, first), (2, 256, 16), allow_negative_indices=False)
    mine = jnp.einsum("ite,itd->ed", own, tokens_near, preferred_element_type=F32).astype(BF)
    other = lax.ppermute(mine, "c", [(0, 1), (1, 0)])
    mine = (mine.astype(F32) + other.astype(F32)).astype(BF)
    mine = added(gathered(mine, "zr", 4).reshape(64, width), 1, 16)
    mine = shifted(mine, group_shift)
    mine, logit_grad, expert_out, slot_grad, rows, hidden, pre_grad = tied(
        mine, logit_grad, expert_out, slot_grad, rows, hidden, pre_grad
    )
    shares = gathered(mine, PLANE, 16).reshape(256, width)
    slots, cotangents = rows[:, :64], rows[:, 64:]
    out_weight_grad = jnp.einsum("erf,erd->efd", hidden, cotangents, preferred_element_type=F32).astype(BF)
    in_weight_grad = jnp.einsum("erd,erf->edf", slots, pre_grad, preferred_element_type=F32).astype(BF)
    weights = jnp.concatenate([dispatch_b, logit_grad], axis=2)
    vectors = jnp.concatenate([slot_grad, jnp.broadcast_to(slot_proj.T, (2, 64, width))], axis=1)
    token_grad = jnp.einsum("itk,ikd->itd", weights, vectors, preferred_element_type=F32).astype(BF)
    mixed = jnp.einsum("ite,ied->itd", combine_b, expert_out, preferred_element_type=F32).astype(BF)
    proj_grad = added(shares, 4, 16).T
    return (mixed, token_grad, proj_grad, in_weight_grad, out_weight_grad)


def solution(mesh):
    fine = Mesh(mesh.devices.reshape(4, 2, 4, 4, 4, 2), ALL)
    images, first, second = P(EXP, None, None), P(EXP, None, REP), P(EXP, REP, None)
    return jax.shard_map(
        on_device,
        mesh=fine,
        in_specs=(images, P(), first, second, images),
        out_specs=(images, images, P(), first, second),
        check_vma=False,
    )
```
